32 devices in a mesh: slab: 4 (over y, core), wall: 8 (over z, x).
Axes of the slice: x: 2, y: 2, z: 4, core: 2. Of those that a mesh axis runs over, the one named last changes fastest.
Arguments:
- flow_state: float32 [64, 5, 32768], P(None, None, ('slab', 'wall')), as said below
- match_elem: int32 [262144], P(('slab', 'wall')), may hold values from 0 to 1023
- match_coord: int32 [3, 262144], P(None, ('slab', 'wall')), may hold values from 0 to 15
- match_dest: int32 [262144, 1], P(('slab', 'wall')), may hold values from 0 to 7; in each aligned block of 8192 rows (0 to 8191, 8192 to 16383, ...) at most 2560 rows name the same one
- roughness: float32 [655360], P(('slab', 'wall')), may hold values from 4 to 30
Outputs:
- rate: float32 [64, 4, 32768], P(None, None, ('slab', 'wall'))
- wall_shear: float32 [2, 655360], P(None, ('slab', 'wall'))
The draws below stay inside these ranges and needn't reach their ends.
Inputs may be any that keep to these rules, and one draw needn't show every extreme that they name: `flow_state`: density lies between 0.8 and 1.25 and the pressure 0.4 (energy - |momentum|^2 / (2 density)) between 0.6 and 1.6 at every node. `match_dest`: among the rows of one device no wall index is named by more than 2560 rows, and in every draw some device names one wall index exactly 2560 times.
All inputs are finite; a program needn't handle non-finite values.
Results may differ from the reference program's by a relative error of at most 0.0003.
Values sent between devices are 32-bit elements; how exact they have to be, the bound alone decides.
A program may use at most 64 MiB of HBM per device.

```python
import math
import jax
import jax.numpy as jnp
import numpy as np
from jax import lax

EX = 4
EY = 2
EZ = 128
RES = 16
NEWTON = 8
E_DEV = 1024
ELEMS = 32768
M_DEV = 8192
MATCH = 262144
CAP = 2560
SLOTS = 655360
N_SLAB = 4
N_WALL = 8


def draw_flow_state(key, part):
    key_rho, key_vel, key_press = jax.random.split(key, 3)
    grid_shape = (64, ELEMS)
    mass_per_volume = jax.random.uniform(key_rho, grid_shape, jnp.float32, 0.8, 1.25)
    stream_speed_vector = jnp.clip(1.5 * jax.random.normal(key_vel, (3, 64, ELEMS), jnp.float32), -4.5, 4.5)
    normal_stress_level = jax.random.uniform(key_press, grid_shape, jnp.float32, 0.6, 1.6)
    momentum = mass_per_volume[None] * stream_speed_vector
    energy = normal_stress_level / 0.4 + 0.5 * mass_per_volume * jnp.sum(stream_speed_vector * stream_speed_vector, axis=0)
    return jnp.stack([mass_per_volume, momentum[0], momentum[1], momentum[2], energy], axis=1)


def set_ends(entries, own_key, least, top_value):
    longest = entries.shape.index(max(entries.shape))
    spots = []
    for shift in (0, 1):
        where = [jax.random.randint(jax.random.fold_in(own_key, axis), (), 0, length) for axis, length in enumerate(entries.shape)]
        where[longest] = (where[longest] + shift) % entries.shape[longest]
        spots.append(tuple(where))
    return entries.at[spots[0]].set(least).at[spots[1]].set(top_value)


def block_scale(rng, shape, cuts, smallest, high):
    factor_of, own = 1.0, jax.random.fold_in(rng, 6)
    for dim, blocks in cuts:
        draws = jnp.exp(jax.random.uniform(jax.random.fold_in(own, dim), (blocks,), jnp.float32, smallest / len(cuts), high / len(cuts)))
        factor_of = factor_of * jnp.repeat(draws, shape[dim] // blocks).reshape([-1 if axis == dim else 1 for axis in range(len(shape))])
    return factor_of


def assign_block(own_key, own, number, rows, amount, top, reach, skew):
    ranking = jax.random.permutation(own_key, amount)
    packed, common = portions_of(amount, rows * top, reach, skew, True), portions_of(amount, rows * top, reach, skew, False)
    places = jnp.arange(amount)

    def named(tallies, turn):
        used = int((tallies > 0).sum())
        fixed = max(1, used // 4)
        passed = fixed + (places - fixed + turn * (used - fixed)) % max(1, amount - fixed)
        return jnp.zeros((amount,), jnp.int32).at[ranking[jnp.where(places < fixed, places, passed)]].set(jnp.asarray(tallies, jnp.int32))

    tallies = jnp.where(number % 4 == 0, named(packed, number // 4), named(common, number - number // 4 - 1))
    mixed = jax.random.permutation(jax.random.fold_in(own, 3), amount)
    donor, receiver = mixed[0:amount // 2 * 2:2], mixed[1:amount // 2 * 2:2]
    margin = jnp.minimum(tallies[donor] - 1, reach - tallies[receiver]) // 2
    margin = jnp.where((donor == ranking[0]) | (receiver == ranking[0]) | (tallies[receiver] == 0), 0, jnp.maximum(margin, 0))
    passed = jax.random.randint(jax.random.fold_in(own, 4), (amount // 2,), 0, 1 << 20) % (margin + 1)
    tallies = tallies.at[donor].add(-passed).at[receiver].add(passed)
    labels = jnp.searchsorted(jnp.cumsum(tallies), jnp.arange(rows * top), side="right").astype(jnp.int32)
    table = labels.reshape(top, rows).T
    table = table[jax.random.permutation(jax.random.fold_in(own, 1), rows)]
    turn = jax.random.randint(jax.random.fold_in(own, 2), (rows, 1), 0, top)
    return jnp.take_along_axis(table, (jnp.arange(top)[None, :] + turn) % top, axis=1)


def portions_of(count, total, reach, lean, full):
    loads = [(1 << 20) // math.isqrt(grade ** lean) + 1 for grade in range(1, count + 1)]
    largest = reach if full else min(reach, max(-(-total // count), total * loads[0] // sum(loads)))
    least = 1 if total - largest >= count - 1 else 0
    counts, spare = [largest] + [least] * (count - 1), total - largest - least * (count - 1)
    while spare > 0:
        free = [i for i in range(1, count) if counts[i] < largest] or [i for i in range(1, count) if counts[i] < reach]
        pool, left = sum([loads[i] for i in free]), spare
        for i in free:
            extra = min(reach - counts[i], max(1, left * loads[i] // pool), spare)
            counts[i] = counts[i] + extra
            spare = spare - extra
    return np.array(counts)


def setup_inputs(seed: int = 0) -> dict:
    keys = jax.random.split(jax.random.key(seed), 6)
    flow_state = draw_flow_state(jax.random.fold_in(keys[5], 71), 0)
    match_elem = set_ends(jax.random.randint(keys[1], (MATCH,), 0, E_DEV), jax.random.fold_in(keys[1], 1), 0, E_DEV - 1).astype(jnp.int32)
    match_coord = set_ends(jax.random.randint(keys[2], (3, MATCH), 0, RES), jax.random.fold_in(keys[2], 1), 0, RES - 1).astype(jnp.int32)
    match_dest_keys = jax.random.split(jax.random.fold_in(keys[3], 1), MATCH // M_DEV)
    match_dest_turns = jax.random.permutation(jax.random.fold_in(keys[3], 3), MATCH // M_DEV)
    match_dest = jax.vmap(lambda own, number: assign_block(jax.random.fold_in(keys[3], 2), own, number, M_DEV, N_WALL, 1, CAP, 1))(match_dest_keys, match_dest_turns).reshape((MATCH, 1))
    roughness = jnp.clip(jnp.exp(math.log(30.0) - 2.014903 * jax.random.uniform(keys[4], (SLOTS,), jnp.float32) ** block_scale(keys[4], (SLOTS,), ((0, 32),), -0.2, 0.2)), 4.0, 30.0)
    return {"flow_state": flow_state, "match_elem": match_elem, "match_coord": match_coord, "match_dest": match_dest, "roughness": roughness}


HIGHEST = lax.Precision.HIGHEST
VISCOSITY = 0.05
FOURIER_LAW_ON = 0.07 / 0.288
KARMAN = 0.41
RELAXATION = 0.35

def gauss_points():
    return np.array([-1.0, -1.0 / np.sqrt(5.0), 1.0 / np.sqrt(5.0), 1.0])

def derivative_tables():
    points = gauss_points()
    bary_weights = np.array([1.0 / np.prod([points[left_index] - points[right_index] for right_index in range(4) if right_index != left_index]) for left_index in range(4)])
    matrix = np.zeros((4, 4))
    for left_index in range(4):
        for right_index in range(4):
            if right_index != left_index:
                matrix[left_index, right_index] = bary_weights[right_index] / bary_weights[left_index] / (points[left_index] - points[right_index])
        matrix[left_index, left_index] = -np.sum(matrix[left_index])
    identity = np.eye(4)
    along_x = np.kron(np.kron(matrix, identity), identity)
    along_y = np.kron(np.kron(identity, matrix), identity)
    along_z = np.kron(np.kron(identity, identity), matrix)
    gradient_table = np.concatenate([along_x, along_y, along_z], axis=0)
    divergence_table = np.concatenate([along_x, along_y, along_z], axis=1)
    return (jnp.asarray(gradient_table, jnp.float32), jnp.asarray(divergence_table, jnp.float32))

def entropy_vars(flow_block, comp_axis):
    mass_per_volume = lax.index_in_dim(flow_block, 0, comp_axis, keepdims=False)
    momentum_x = lax.index_in_dim(flow_block, 1, comp_axis, keepdims=False)
    momentum_y = lax.index_in_dim(flow_block, 2, comp_axis, keepdims=False)
    momentum_z = lax.index_in_dim(flow_block, 3, comp_axis, keepdims=False)
    energy = lax.index_in_dim(flow_block, 4, comp_axis, keepdims=False)
    speed_sq = momentum_x * momentum_x + momentum_y * momentum_y + momentum_z * momentum_z
    normal_stress_level = 0.4 * (energy - 0.5 * speed_sq / mass_per_volume)
    entropy_s = jnp.log(normal_stress_level) - 1.4 * jnp.log(mass_per_volume)
    leading = (1.4 - entropy_s) / 0.4 - 0.5 * speed_sq / (mass_per_volume * normal_stress_level)
    return jnp.stack([leading, momentum_x / normal_stress_level, momentum_y / normal_stress_level, momentum_z / normal_stress_level, -mass_per_volume / normal_stress_level], comp_axis)

def face_terms(field_view, node_axis, elem_axis, lower_edge, upper_edge):
    lower_face = lax.index_in_dim(field_view, 0, node_axis, keepdims=False)
    upper_face = lax.index_in_dim(field_view, 3, node_axis, keepdims=False)
    extent = lower_face.shape[elem_axis]
    next_lower = jnp.concatenate([lax.slice_in_dim(lower_face, 1, extent, axis=elem_axis), upper_edge], elem_axis)
    prev_upper = jnp.concatenate([lower_edge, lax.slice_in_dim(upper_face, 0, extent - 1, axis=elem_axis)], elem_axis)
    add_lower = -3.0 * (prev_upper - lower_face)
    add_upper = 3.0 * (next_lower - upper_face)
    nothing = jnp.zeros_like(lower_face)
    return jnp.stack([add_lower, nothing, nothing, add_upper], node_axis)

def own_terms(field_view, node_axis, elem_axis):
    lower_face = lax.index_in_dim(field_view, 0, node_axis, keepdims=False)
    upper_face = lax.index_in_dim(field_view, 3, node_axis, keepdims=False)
    extent = lower_face.shape[elem_axis]
    return face_terms(field_view, node_axis, elem_axis, lax.slice_in_dim(lower_face, 0, 1, axis=elem_axis), lax.slice_in_dim(upper_face, extent - 1, extent, axis=elem_axis))

def edge_packs(field_x, field_z):
    lower_x = field_x[0]
    upper_x = field_x[3]
    pack_x = jnp.stack([lower_x[:, :, :, 0], upper_x[:, :, :, -1]], 0)
    lower_z = field_z[:, :, 0]
    upper_z = field_z[:, :, 3]
    pack_z = jnp.stack([lower_z[..., 0], upper_z[..., -1]], 0)
    return (pack_x, pack_z)

def viscous_flux(flow_block, entropy_view, edge_faces, tables):
    elem_count = EX * EY * EZ
    nodal_derivs = jnp.dot(tables[0], entropy_view.reshape(64, 5 * elem_count), precision=HIGHEST, preferred_element_type=jnp.float32).reshape(3, 4, 4, 4, 5, EX, EY, EZ)
    lower_x, upper_x, lower_z, upper_z = edge_faces
    recovered_slopes = [nodal_derivs[0] + face_terms(entropy_view, 0, 3, lower_x, upper_x), nodal_derivs[1] + own_terms(entropy_view, 1, 4), nodal_derivs[2] + face_terms(entropy_view, 2, 5, lower_z, upper_z)]
    conserved = flow_block.reshape(4, 4, 4, 5, EX, EY, EZ)
    mass_per_volume = conserved[:, :, :, 0]
    stream_speed_vector = [conserved[:, :, :, 1] / mass_per_volume, conserved[:, :, :, 2] / mass_per_volume, conserved[:, :, :, 3] / mass_per_volume]
    speed_sq = mass_per_volume * (stream_speed_vector[0] * stream_speed_vector[0] + stream_speed_vector[1] * stream_speed_vector[1] + stream_speed_vector[2] * stream_speed_vector[2])
    normal_stress_level = 0.4 * (conserved[:, :, :, 4] - 0.5 * speed_sq)
    kelvin_level = normal_stress_level / mass_per_volume
    strain_rate_tensor = [[kelvin_level * (recovered_slopes[coordinate_heading][:, :, :, 1 + matrix_entry_position] + stream_speed_vector[matrix_entry_position] * recovered_slopes[coordinate_heading][:, :, :, 4]) for matrix_entry_position in range(3)] for coordinate_heading in range(3)]
    divergence = strain_rate_tensor[0][0] + strain_rate_tensor[1][1] + strain_rate_tensor[2][2]
    fluxes = []
    for coordinate_heading in range(3):
        stress = []
        for matrix_entry_position in range(3):
            stress_entry = VISCOSITY * (strain_rate_tensor[coordinate_heading][matrix_entry_position] + strain_rate_tensor[matrix_entry_position][coordinate_heading])
            if matrix_entry_position == coordinate_heading:
                stress_entry = stress_entry - 2.0 / 3.0 * VISCOSITY * divergence
            stress.append(stress_entry)
        enthalpy_transport = FOURIER_LAW_ON * kelvin_level * kelvin_level * recovered_slopes[coordinate_heading][:, :, :, 4]
        energy_flux = stream_speed_vector[0] * stress[0] + stream_speed_vector[1] * stress[1] + stream_speed_vector[2] * stress[2] + enthalpy_transport
        fluxes.append(jnp.stack([stress[0], stress[1], stress[2], energy_flux], 3))
    return fluxes

def residual_rate(fluxes, edge_faces, stress_rows, tables):
    elem_count = EX * EY * EZ
    stacked = jnp.stack(fluxes, 0).reshape(192, 4 * elem_count)
    rate_field = jnp.dot(tables[1], stacked, precision=HIGHEST, preferred_element_type=jnp.float32).reshape(4, 4, 4, 4, EX, EY, EZ)
    lower_x, upper_x, lower_z, upper_z = edge_faces
    rate_field = rate_field + face_terms(fluxes[0], 0, 3, lower_x, upper_x) + own_terms(fluxes[1], 1, 4) + face_terms(fluxes[2], 2, 5, lower_z, upper_z)
    shear_rows = stress_rows.reshape(2, 4, 4, EX, EZ)
    bottom = fluxes[1][:, 0, :, :, :, 0, :]
    rate_field = rate_field.at[:, 0, :, 0, :, 0, :].add(6.0 * (bottom[:, :, 0] - shear_rows[0]))
    rate_field = rate_field.at[:, 0, :, 2, :, 0, :].add(6.0 * (bottom[:, :, 2] - shear_rows[1]))
    return rate_field.reshape(64, 4, elem_count)

def lagrange_rows(coordinate):
    points = gauss_points()
    rows_out = []
    for left_index in range(4):
        factor_prod = jnp.ones_like(coordinate)
        for right_index in range(4):
            if right_index != left_index:
                factor_prod = factor_prod * (coordinate - float(points[right_index])) / float(points[left_index] - points[right_index])
        rows_out.append(factor_prod)
    return jnp.stack(rows_out, 0)

def probe_values(flow_block, elements, coords_int):
    coords = (2.0 * coords_int.astype(jnp.float32) + 1.0) / RES - 1.0
    basis_x = lagrange_rows(coords[0])
    basis_y = lagrange_rows(coords[1])
    basis_z = lagrange_rows(coords[2])
    weights = (basis_x[:, None, None, :] * basis_y[None, :, None, :] * basis_z[None, None, :, :]).reshape(64, -1)
    values = [lax.optimization_barrier(jnp.sum(weights * jnp.take(flow_block[:, matrix_entry_position, :], elements, axis=1), axis=0)) for matrix_entry_position in (0, 1, 3)]
    layer_index = (elements // EZ % EY).astype(jnp.float32)
    return jnp.stack(values + [2.0 * layer_index + 1.0 + coords[1]], 0)

def slot_ranks(destination, wall_count):
    onehot = (destination[None, :] == jnp.arange(wall_count, dtype=jnp.int32)[:, None]).astype(jnp.int32)
    before = jnp.cumsum(onehot, axis=1) - onehot
    return lax.optimization_barrier(jnp.sum(before * onehot, axis=0)).astype(jnp.int32)

def wall_model(mass_per_volume, mom_x, mom_z, height, factor):
    vel_x = mom_x / mass_per_volume
    vel_z = mom_z / mass_per_volume
    slip_speed = jnp.maximum(jnp.sqrt(vel_x * vel_x + vel_z * vel_z), 0.5)
    reynolds = height * slip_speed * mass_per_volume / VISCOSITY
    log_term = jnp.log(factor * reynolds)
    newton_ratio = jnp.ones_like(mass_per_volume)
    for sweep_index in range(NEWTON):
        residue = newton_ratio - (log_term - jnp.log(newton_ratio)) / KARMAN
        newton_slope = 1.0 + 1.0 / (KARMAN * newton_ratio)
        newton_ratio = newton_ratio - RELAXATION * residue / newton_slope
    friction = slip_speed / newton_ratio
    stress_scale = mass_per_volume * friction * friction / slip_speed
    return (stress_scale * vel_x, stress_scale * vel_z)

def reference(flow_state, match_elem, match_coord, match_dest, roughness):
    tables = derivative_tables()
    devices = N_SLAB * N_WALL
    destination_all = match_dest[:, 0]

    def block_of(device):
        return lax.dynamic_slice_in_dim(flow_state, device * E_DEV, E_DEV, axis=2)

    def rows_of(source, device):
        return lax.dynamic_slice_in_dim(source, device * M_DEV, M_DEV, axis=source.ndim - 1)

    def neighbours(device):
        slab_pos = device // N_WALL
        wall_pos = device % N_WALL
        prev_x = (slab_pos + N_SLAB - 1) % N_SLAB * N_WALL + wall_pos
        next_x = (slab_pos + 1) % N_SLAB * N_WALL + wall_pos
        prev_z = slab_pos * N_WALL + (wall_pos + N_WALL - 1) % N_WALL
        next_z = slab_pos * N_WALL + (wall_pos + 1) % N_WALL
        return (prev_x, next_x, prev_z, next_z)

    def edges_from(packs_x, packs_z, device):
        prev_x, next_x, prev_z, next_z = neighbours(device)
        return (packs_x[prev_x][1][:, :, :, None], packs_x[next_x][0][:, :, :, None], packs_z[prev_z][1][..., None], packs_z[next_z][0][..., None])

    def first_pass(device, loop_carry):
        packs_x, packs_z, probes, slots = loop_carry
        device = device.astype(jnp.int32)
        flow_block = block_of(device)
        entropy_view = entropy_vars(flow_block, 1).reshape(4, 4, 4, 5, EX, EY, EZ)
        pack_x, pack_z = edge_packs(entropy_view, entropy_view)
        probe_rows = probe_values(flow_block, rows_of(match_elem, device), rows_of(match_coord, device))
        destination = rows_of(destination_all, device)
        slot_rank = slot_ranks(destination, N_WALL)
        slot_index = (device // N_WALL * N_WALL + destination) * (N_WALL * CAP) + device % N_WALL * CAP + slot_rank
        return (packs_x.at[device].set(pack_x), packs_z.at[device].set(pack_z), lax.dynamic_update_slice_in_dim(probes, probe_rows, device * M_DEV, axis=1), lax.dynamic_update_slice_in_dim(slots, slot_index.astype(jnp.int32), device * M_DEV, axis=0))
    start_carry = (jnp.zeros((devices, 2, 4, 4, 5, EY, EZ), jnp.float32), jnp.zeros((devices, 2, 4, 4, 5, EX, EY), jnp.float32), jnp.zeros((4, MATCH), jnp.float32), jnp.zeros((MATCH,), jnp.int32))
    packs_x, packs_z, probes, slots = lax.fori_loop(0, devices, first_pass, start_carry)
    slot_data = jnp.zeros((4, SLOTS), jnp.float32).at[:, slots].set(probes)
    occupied = slot_data[0] > 0.0
    mass_per_volume = jnp.where(occupied, slot_data[0], 1.0)
    height = jnp.where(occupied, slot_data[3], 1.0)
    stress_x, stress_z = wall_model(mass_per_volume, slot_data[1], slot_data[2], height, roughness)
    wall_shear = jnp.where(occupied[None, :], jnp.stack([stress_x, stress_z], 0), 0.0)

    def flux_of(device):
        flow_block = block_of(device)
        entropy_view = entropy_vars(flow_block, 1).reshape(4, 4, 4, 5, EX, EY, EZ)
        return viscous_flux(flow_block, entropy_view, edges_from(packs_x, packs_z, device), tables)

    def second_pass(device, loop_carry):
        flux_x, flux_z = loop_carry
        device = device.astype(jnp.int32)
        fluxes = flux_of(device)
        pack_x, pack_z = edge_packs(fluxes[0], fluxes[2])
        return (flux_x.at[device].set(pack_x), flux_z.at[device].set(pack_z))
    flux_x, flux_z = lax.fori_loop(0, devices, second_pass, (jnp.zeros((devices, 2, 4, 4, 4, EY, EZ), jnp.float32), jnp.zeros((devices, 2, 4, 4, 4, EX, EY), jnp.float32)))

    def third_pass(device, rate_all):
        device = device.astype(jnp.int32)
        fluxes = flux_of(device)
        stress_rows = wall_shear[:, rows_of(slots, device)]
        rate_field = residual_rate(fluxes, edges_from(flux_x, flux_z, device), stress_rows, tables)
        return lax.dynamic_update_slice_in_dim(rate_all, rate_field, device * E_DEV, axis=2)
    rate_all = lax.fori_loop(0, devices, third_pass, jnp.zeros((64, 4, ELEMS), jnp.float32))
    return (rate_all, wall_shear)
```

```python
import jax
import jax.numpy as jnp
import numpy as np
from jax import lax
from jax.experimental import pallas as pl
from jax.experimental.pallas import tpu as pltpu
from jax.sharding import PartitionSpec as P

EX = 4
EY = 2
EZ = 128
ROWS = EX * EY
RES = 16
NEWTON = 8
LANES = 128
WIDTH = 512
VISCOSITY = 0.05
FOURIER_LAW_ON = 0.07 / 0.288
KARMAN = 0.41
RELAXATION = 0.35
F32 = jnp.float32
BF16 = jnp.bfloat16
PARAMS = pltpu.CompilerParams(vmem_limit_bytes=48 * 2**20)
VMEM = pl.BlockSpec(memory_space=pltpu.VMEM)
ANY = pl.BlockSpec(memory_space=pl.ANY)


def gauss_points():
    return np.array([-1.0, -1.0 / np.sqrt(5.0), 1.0 / np.sqrt(5.0), 1.0])


def derivative_matrix():
    points = gauss_points()
    weights = [
        1.0 / np.prod([points[i] - points[j] for j in range(4) if j != i]) for i in range(4)
    ]
    matrix = np.zeros((4, 4))
    for i in range(4):
        for j in range(4):
            if j != i:
                matrix[i, j] = weights[j] / weights[i] / (points[i] - points[j])
        matrix[i, i] = -np.sum(matrix[i])
    return matrix


TABLE = derivative_matrix() + np.diag([3.0, 0.0, 0.0, -3.0])


def line_slopes(values, prev_upper, next_lower):
    outs = []
    for i in range(4):
        total = None
        for j in range(4):
            coef = float(TABLE[i, j])
            if abs(coef) > 1e-12:
                term = coef * values[j]
                total = term if total is None else total + term
        if i == 0:
            total = total - 3.0 * prev_upper
        if i == 3:
            total = total + 3.0 * next_lower
        outs.append(total)
    return outs


def tile_iota(axis):
    return lax.broadcasted_iota(jnp.int32, (ROWS, EZ), axis)


def x_line(source, i, comp, edges):
    row = tile_iota(0)
    values = [source[16 * a + i, comp] for a in range(4)]
    edge = edges[i, comp % 4]
    prev_upper = jnp.where(row < EY, edge, pltpu.roll(values[3], EY, 0))
    next_lower = jnp.where(row >= ROWS - EY, edge, pltpu.roll(values[0], ROWS - EY, 0))
    return line_slopes(values, prev_upper, next_lower)


def y_line(source, i, comp):
    layer = tile_iota(0) % EY
    base = 16 * (i // 4) + i % 4
    values = [source[base + 4 * b, comp] for b in range(4)]
    prev_upper = jnp.where(layer > 0, pltpu.roll(values[3], 1, 0), values[0])
    next_lower = jnp.where(layer < EY - 1, pltpu.roll(values[0], ROWS - 1, 0), values[3])
    return values, line_slopes(values, prev_upper, next_lower)


def z_line(source, i, comp, low, high):
    lane = tile_iota(1)
    values = [source[4 * i + c, comp] for c in range(4)]
    prev_upper = jnp.where(lane == 0, low, pltpu.roll(values[3], 1, 1))
    next_lower = jnp.where(lane == EZ - 1, high, pltpu.roll(values[0], EZ - 1, 1))
    return line_slopes(values, prev_upper, next_lower)


def write_edges(source, comp_x, comp_z, edge_x, edge_z):
    edge_x[0] = source[0:16, comp_x : comp_x + 4, 0:EY, :]
    edge_x[1] = source[48:64, comp_x : comp_x + 4, ROWS - EY : ROWS, :]
    lane = tile_iota(1)

    def pack(i, carry):
        low, high = carry
        for comp in range(4):
            here = lane == 4 * i + comp
            low = jnp.where(here, source[4 * i, comp_z + comp][:, 0:1], low)
            high = jnp.where(here, source[4 * i + 3, comp_z + comp][:, EZ - 1 : EZ], high)
        return low, high

    zero = jnp.zeros((ROWS, EZ), F32)
    low, high = lax.fori_loop(0, 16, pack, (zero, zero), unroll=4)
    edge_z[0] = low
    edge_z[1] = high


def entropy_kernel(flow, ent, prim, edge_x, edge_z, held, sems):
    copies = [
        pltpu.make_async_copy(
            flow.at[:, :, pl.ds(k * EZ, EZ)], held.at[:, :, k, :], sems.at[k]
        )
        for k in range(ROWS)
    ]
    for copy in copies:
        copy.start()
    for copy in copies:
        copy.wait()

    def node(n, carry):
        rho, mx, my, mz, energy = [held[n, k] for k in range(5)]
        inv_rho = 1.0 / rho
        pressure = 0.4 * (energy - 0.5 * (mx * mx + my * my + mz * mz) * inv_rho)
        inv_p = 1.0 / pressure
        ent[n, 0] = mx * inv_p
        ent[n, 1] = my * inv_p
        ent[n, 2] = mz * inv_p
        ent[n, 3] = -rho * inv_p
        prim[n, 0] = mx * inv_rho
        prim[n, 1] = my * inv_rho
        prim[n, 2] = mz * inv_rho
        prim[n, 3] = pressure * inv_rho
        return carry

    lax.fori_loop(0, 64, node, 0, unroll=4)
    write_edges(ent, 0, 0, edge_x, edge_z)


def fill_edges(edges, low_x, high_x):
    edges[:, :, 0:EY, :] = low_x[...]
    edges[:, :, ROWS - EY : ROWS, :] = high_x[...]


def flux_kernel(ent, prim, low_x, high_x, low_z, high_z, flux, edge_x, edge_z, edges):
    fill_edges(edges, low_x, high_x)

    def lines(i, carry):
        low, high = carry
        for comp in range(4):
            for a, value in enumerate(x_line(ent, i, comp, edges)):
                flux[16 * a + i, comp] = value
            for b, value in enumerate(y_line(ent, i, comp)[1]):
                flux[16 * (i // 4) + 4 * b + i % 4, 4 + comp] = value
            outs = z_line(ent, i, comp, low[:, comp : comp + 1], high[:, comp : comp + 1])
            for c, value in enumerate(outs):
                flux[4 * i + c, 8 + comp] = value
        return pltpu.roll(low, EZ - 4, 1), pltpu.roll(high, EZ - 4, 1)

    lax.fori_loop(0, 16, lines, (low_z[...], high_z[...]))

    def node(n, carry):
        vel = [prim[n, k] for k in range(3)]
        temp = prim[n, 3]
        slope4 = [flux[n, 4 * d + 3] for d in range(3)]
        strain = [
            [temp * (flux[n, 4 * d + i] + vel[i] * slope4[d]) for i in range(3)]
            for d in range(3)
        ]
        bulk = (2.0 / 3.0 * VISCOSITY) * (strain[0][0] + strain[1][1] + strain[2][2])
        heat = FOURIER_LAW_ON * temp * temp
        tau = {}
        for d in range(3):
            for i in range(d, 3):
                entry = VISCOSITY * (strain[d][i] + strain[i][d])
                if i == d:
                    entry = entry - bulk
                tau[d, i] = tau[i, d] = entry
        for d in range(3):
            for i in range(3):
                flux[n, 4 * d + i] = tau[i, d]
            flux[n, 4 * d + 3] = (
                vel[0] * tau[0, d] + vel[1] * tau[1, d] + vel[2] * tau[2, d] + heat * slope4[d]
            )
        return carry

    lax.fori_loop(0, 64, node, 0, unroll=2)
    write_edges(flux, 0, 8, edge_x, edge_z)


def rate_kernel(flux, low_x, high_x, low_z, high_z, shear, rate, edges, held, sems):
    fill_edges(edges, low_x, high_x)

    def lines_x(i, carry):
        for comp in range(4):
            for a, value in enumerate(x_line(flux, i, comp, edges)):
                held[16 * a + i, comp] = value
        return carry

    lax.fori_loop(0, 16, lines_x, 0, unroll=2)
    row = tile_iota(0)

    def lines_y(i, carry):
        for comp in range(4):
            values, outs = y_line(flux, i, 4 + comp)
            if comp in (0, 2):
                wall = jnp.zeros((ROWS, EZ), F32)
                for ex in range(EX):
                    here = shear[comp // 2, pl.ds(EX * i + ex, 1), :]
                    wall = jnp.where(row == EY * ex, 6.0 * (values[0] - here), wall)
                outs[0] = outs[0] + wall
            for b, value in enumerate(outs):
                held[16 * (i // 4) + 4 * b + i % 4, comp] += value
        return carry

    lax.fori_loop(0, 16, lines_y, 0, unroll=2)

    def lines_z(i, carry):
        low, high = carry
        for comp in range(4):
            outs = z_line(flux, i, 8 + comp, low[:, comp : comp + 1], high[:, comp : comp + 1])
            for c, value in enumerate(outs):
                held[4 * i + c, comp] += value
        return pltpu.roll(low, EZ - 4, 1), pltpu.roll(high, EZ - 4, 1)

    lax.fori_loop(0, 16, lines_z, (low_z[...], high_z[...]), unroll=2)
    copies = [
        pltpu.make_async_copy(
            held.at[:, :, k, :], rate.at[:, :, pl.ds(k * EZ, EZ)], sems.at[k]
        )
        for k in range(ROWS)
    ]
    for copy in copies:
        copy.start()
    for copy in copies:
        copy.wait()


def two_parts(value):
    high = value.astype(BF16)
    return high, (value - high.astype(F32)).astype(BF16)


def hot(rows, index):
    ids = lax.broadcasted_iota(jnp.int32, (rows, index.shape[1]), 0)
    return jnp.where(ids == index, 1.0, 0.0).astype(BF16)


def lanes(ref, first, count):
    return jnp.concatenate([ref[pl.ds(first + j, 1), :] for j in range(count)], axis=1)


def lagrange_rows(coordinate):
    points = gauss_points()
    rows_out = []
    for i in range(4):
        product = None
        scale = 1.0
        for j in range(4):
            if j != i:
                factor = coordinate - float(points[j])
                product = factor if product is None else product * factor
                scale = scale / (points[i] - points[j])
        rows_out.append(product * float(scale))
    return rows_out


def slot_numbers(dest, wall_count, capacity):
    rows = dest.shape[0]
    masks = [jnp.where(dest == w, 1.0, 0.0) for w in range(wall_count)]
    stacked = jnp.concatenate([mask.astype(BF16) for mask in masks], axis=0)
    from_lane = lax.broadcasted_iota(jnp.int32, (LANES, 2 * LANES), 0)
    to_lane = lax.broadcasted_iota(jnp.int32, (LANES, 2 * LANES), 1)
    upper = jnp.where(from_lane < to_lane, 1.0, 0.0).astype(BF16)
    counts = jnp.dot(stacked, upper, preferred_element_type=F32)
    from_row = lax.broadcasted_iota(jnp.int32, (rows, rows), 1)
    to_row = lax.broadcasted_iota(jnp.int32, (rows, rows), 0)
    below = jnp.where(from_row < to_row, 1.0, 0.0).astype(BF16)
    rank = jnp.zeros(dest.shape, F32)
    for w in range(wall_count):
        part = counts[w * rows : (w + 1) * rows]
        earlier = jnp.dot(below, part[:, LANES:].astype(BF16), preferred_element_type=F32)
        rank = rank + masks[w] * (part[:, :LANES] + earlier)
    return dest * capacity + rank.astype(jnp.int32)


def wall_model(mass_per_volume, mom_x, mom_z, height, factor):
    vel_x = mom_x / mass_per_volume
    vel_z = mom_z / mass_per_volume
    slip_speed = jnp.maximum(jnp.sqrt(vel_x * vel_x + vel_z * vel_z), 0.5)
    reynolds = height * slip_speed * mass_per_volume / VISCOSITY
    log_term = jnp.log(factor * reynolds)
    ratio = jnp.ones_like(mass_per_volume)
    for sweep_index in range(NEWTON):
        residue = ratio - (log_term - jnp.log(ratio)) / KARMAN
        newton_slope = 1.0 + 1.0 / (KARMAN * ratio)
        ratio = ratio - RELAXATION * residue / newton_slope
    friction = slip_speed / ratio
    stress_scale = mass_per_volume * friction * friction / slip_speed
    return (stress_scale * vel_x, stress_scale * vel_z)


def wall_kernel(
    wall_count, flow, elem, coord, dest, rough, shear, outgoing,
    columns, parts, slots, probe, total, sems,
):
    copies = [
        pltpu.make_async_copy(flow.at[:, comp, :], columns.at[k], sems.at[k])
        for k, comp in enumerate((0, 1, 3))
    ]
    for copy in copies:
        copy.start()
    rows = elem.shape[0]
    grid_rows = rough.shape[0]
    elems = columns.shape[2]
    slots[...] = slot_numbers(dest[...], wall_count, grid_rows * LANES // wall_count)
    table = jnp.concatenate(two_parts(rough[...]), axis=0)
    for copy in copies:
        copy.wait()
    for k in range(3):
        high, low = two_parts(columns[k])
        parts[64 * k : 64 * k + 64] = high
        parts[192 + 64 * k : 256 + 64 * k] = low
    group = WIDTH // LANES

    def probe_block(t, carry):
        first = group * t
        element = lanes(elem, first, group)
        slot = lanes(slots, first, group)
        coords = coord[:, pl.ds(pl.multiple_of(t * WIDTH, WIDTH), WIDTH)]
        coords = (2.0 * coords.astype(F32) + 1.0) / RES - 1.0
        inner = hot(LANES, element % LANES)
        pieces = []
        for g in range(elems // LANES):
            pick = jnp.where(element // LANES == g, 1.0, 0.0).astype(BF16)
            pieces.append(inner * pick)
        element_hot = jnp.concatenate(pieces, axis=0)
        picked = jnp.dot(parts[...], element_hot, preferred_element_type=F32)
        picked = picked[:192] + picked[192:]
        basis = lagrange_rows(coords)
        along_z = jnp.concatenate([basis[c][2:3] for c in range(4)], axis=0)
        plane = jnp.concatenate([basis[b][1:2] * along_z for b in range(4)], axis=0)
        outs = []
        for k in range(3):
            mixed = basis[0][0:1] * picked[64 * k : 64 * k + 16]
            for a in range(1, 4):
                mixed = mixed + basis[a][0:1] * picked[64 * k + 16 * a : 64 * k + 16 * a + 16]
            outs.append(jnp.sum(mixed * plane, axis=0, keepdims=True))
        layer = (element // EZ % EY).astype(F32)
        outs.append(2.0 * layer + 1.0 + coords[1:2])
        found = jnp.dot(table, hot(LANES, slot % LANES), preferred_element_type=F32)
        found = found[:grid_rows] + found[grid_rows:]
        ids = lax.broadcasted_iota(jnp.int32, (grid_rows, WIDTH), 0)
        outs.append(
            jnp.sum(jnp.where(ids == slot // LANES, found, 0.0), axis=0, keepdims=True)
        )
        for k, value in enumerate(outs):
            for j in range(group):
                probe[k, pl.ds(first + j, 1), :] = value[:, LANES * j : LANES * (j + 1)]
        return carry

    lax.fori_loop(0, rows // group, probe_block, 0)
    stress = wall_model(probe[0], probe[1], probe[2], probe[3], probe[4])
    shear[0] = stress[0]
    shear[1] = stress[1]
    total[...] = jnp.zeros_like(total)

    def scatter_block(t, carry):
        first = group * t
        slot = lanes(slots, first, group)
        owner = hot(grid_rows, slot // LANES)
        left = []
        for s in range(2):
            for part in two_parts(lanes(shear.at[s], first, group)):
                left.append(owner * part)
        total[...] += lax.dot_general(
            jnp.concatenate(left, axis=0),
            hot(LANES, slot % LANES),
            (((1,), (1,)), ((), ())),
            preferred_element_type=F32,
        )
        return carry

    lax.fori_loop(0, rows // group, scatter_block, 0)
    for s in range(2):
        base = 2 * s * grid_rows
        outgoing[s] = total[base : base + grid_rows] + total[base + grid_rows : base + 2 * grid_rows]


def shape(*dims):
    return jax.ShapeDtypeStruct(dims, F32)


def exchange(edge_x, edge_z):
    outs = []
    for axis, packs in (("slab", edge_x), ("wall", edge_z)):
        count = lax.axis_size(axis)
        forward = [(i, (i + 1) % count) for i in range(count)]
        backward = [(target, source) for source, target in forward]
        outs.append(lax.ppermute(packs[1], axis, forward))
        outs.append(lax.ppermute(packs[0], axis, backward))
    return outs


def local(flow_state, match_elem, match_coord, match_dest, roughness):
    wall_count = lax.axis_size("wall")
    count = match_elem.shape[0]
    rows = count // LANES
    grid_rows = roughness.shape[0] // LANES
    elems = flow_state.shape[2]
    edge_shapes = (shape(2, 16, 4, EY, EZ), shape(2, ROWS, EZ))
    rough = lax.all_to_all(
        roughness.reshape(grid_rows, LANES), "wall", split_axis=0, concat_axis=0, tiled=True
    )
    ent, prim, edge_x, edge_z = pl.pallas_call(
        entropy_kernel,
        out_shape=(shape(64, 4, ROWS, EZ), shape(64, 4, ROWS, EZ)) + edge_shapes,
        in_specs=[ANY],
        out_specs=[VMEM] * 4,
        scratch_shapes=[pltpu.VMEM((64, 5, ROWS, EZ), F32), pltpu.SemaphoreType.DMA((ROWS,))],
        compiler_params=PARAMS,
        name="entropy_step",
    )(flow_state)
    low_x, high_x, low_z, high_z = exchange(edge_x, edge_z)
    shear, outgoing = pl.pallas_call(
        lambda *refs: wall_kernel(wall_count, *refs),
        out_shape=(shape(2, rows, LANES), shape(2, grid_rows, LANES)),
        in_specs=[ANY] + [VMEM] * 4,
        out_specs=[VMEM] * 2,
        scratch_shapes=[
            pltpu.VMEM((3, 64, elems), F32),
            pltpu.VMEM((384, elems), BF16),
            pltpu.VMEM((rows, LANES), jnp.int32),
            pltpu.VMEM((5, rows, LANES), F32),
            pltpu.VMEM((4 * grid_rows, LANES), F32),
            pltpu.SemaphoreType.DMA((3,)),
        ],
        compiler_params=PARAMS,
        cost_estimate=pl.CostEstimate(
            flops=2 * 384 * elems * count, bytes_accessed=4 * 192 * elems, transcendentals=0
        ),
        name="wall_step",
    )(
        flow_state,
        match_elem.reshape(rows, LANES),
        match_coord,
        match_dest.reshape(rows, LANES),
        rough,
    )
    wall_shear = lax.all_to_all(outgoing, "wall", split_axis=1, concat_axis=1, tiled=True)
    flux, edge_x, edge_z = pl.pallas_call(
        flux_kernel,
        out_shape=(shape(64, 12, ROWS, EZ),) + edge_shapes,
        in_specs=[VMEM] * 6,
        out_specs=[VMEM] * 3,
        scratch_shapes=[pltpu.VMEM((16, 4, ROWS, EZ), F32)],
        compiler_params=PARAMS,
        name="flux_step",
    )(ent, prim, low_x, high_x, low_z, high_z)
    low_x, high_x, low_z, high_z = exchange(edge_x, edge_z)
    rate = pl.pallas_call(
        rate_kernel,
        out_shape=shape(64, 4, elems),
        in_specs=[VMEM] * 6,
        out_specs=ANY,
        scratch_shapes=[
            pltpu.VMEM((16, 4, ROWS, EZ), F32),
            pltpu.VMEM((64, 4, ROWS, EZ), F32),
            pltpu.SemaphoreType.DMA((ROWS,)),
        ],
        compiler_params=PARAMS,
        name="rate_step",
    )(flux, low_x, high_x, low_z, high_z, shear)
    return (rate, wall_shear.reshape(2, grid_rows * LANES))


def solution(mesh):
    return jax.shard_map(
        local,
        mesh=mesh,
        in_specs=(
            P(None, None, ("slab", "wall")),
            P(("slab", "wall")),
            P(None, ("slab", "wall")),
            P(("slab", "wall"), None),
            P(("slab", "wall")),
        ),
        out_specs=(P(None, None, ("slab", "wall")), P(None, ("slab", "wall"))),
        check_vma=False,
    )
```

```python
import jax
import jax.numpy as jnp
import numpy as np
from jax import lax
from jax.experimental import pallas as pl
from jax.experimental.pallas import tpu as pltpu
from jax.sharding import PartitionSpec as P

EX = 4
EY = 2
EZ = 128
ROWS = EX * EY
RES = 16
NEWTON = 8
LANES = 128
WIDTH = 512
VISCOSITY = 0.05
FOURIER_LAW_ON = 0.07 / 0.288
KARMAN = 0.41
RELAXATION = 0.35
F32 = jnp.float32
BF16 = jnp.bfloat16
MESH = pl.DeviceIdType.MESH
VMEM = pl.BlockSpec(memory_space=pltpu.VMEM)
ANY = pl.BlockSpec(memory_space=pl.ANY)


def gauss_points():
    return np.array([-1.0, -1.0 / np.sqrt(5.0), 1.0 / np.sqrt(5.0), 1.0])


def derivative_matrix():
    points = gauss_points()
    weights = [
        1.0 / np.prod([points[i] - points[j] for j in range(4) if j != i]) for i in range(4)
    ]
    matrix = np.zeros((4, 4))
    for i in range(4):
        for j in range(4):
            if j != i:
                matrix[i, j] = weights[j] / weights[i] / (points[i] - points[j])
        matrix[i, i] = -np.sum(matrix[i])
    return matrix


TABLE = derivative_matrix() + np.diag([3.0, 0.0, 0.0, -3.0])


def line_slopes(values, prev_upper, next_lower):
    outs = []
    for i in range(4):
        total = None
        for j in range(4):
            coef = float(TABLE[i, j])
            if abs(coef) > 1e-12:
                term = coef * values[j]
                total = term if total is None else total + term
        if i == 0:
            total = total - 3.0 * prev_upper
        if i == 3:
            total = total + 3.0 * next_lower
        outs.append(total)
    return outs


def tile_iota(axis):
    return lax.broadcasted_iota(jnp.int32, (ROWS, EZ), axis)


def x_line(source, i, comp, edges):
    row = tile_iota(0)
    values = [source[16 * a + i, comp] for a in range(4)]
    edge = edges[i, comp % 4]
    prev_upper = jnp.where(row < EY, edge, pltpu.roll(values[3], EY, 0))
    next_lower = jnp.where(row >= ROWS - EY, edge, pltpu.roll(values[0], ROWS - EY, 0))
    return line_slopes(values, prev_upper, next_lower)


def y_line(source, i, comp):
    layer = tile_iota(0) % EY
    base = 16 * (i // 4) + i % 4
    values = [source[base + 4 * b, comp] for b in range(4)]
    prev_upper = jnp.where(layer > 0, pltpu.roll(values[3], 1, 0), values[0])
    next_lower = jnp.where(layer < EY - 1, pltpu.roll(values[0], ROWS - 1, 0), values[3])
    return values, line_slopes(values, prev_upper, next_lower)


def z_line(source, i, comp, low, high):
    lane = tile_iota(1)
    values = [source[4 * i + c, comp] for c in range(4)]
    prev_upper = jnp.where(lane == 0, low, pltpu.roll(values[3], 1, 1))
    next_lower = jnp.where(lane == EZ - 1, high, pltpu.roll(values[0], EZ - 1, 1))
    return line_slopes(values, prev_upper, next_lower)


def write_edges(source, comp_x, comp_z, edge_x, edge_z):
    edge_x[0] = source[0:16, comp_x : comp_x + 4, 0:EY, :]
    edge_x[1] = source[48:64, comp_x : comp_x + 4, ROWS - EY : ROWS, :]
    lane = tile_iota(1)

    def pack(i, carry):
        low, high = carry
        for comp in range(4):
            here = lane == 4 * i + comp
            low = jnp.where(here, source[4 * i, comp_z + comp][:, 0:1], low)
            high = jnp.where(here, source[4 * i + 3, comp_z + comp][:, EZ - 1 : EZ], high)
        return low, high

    zero = jnp.zeros((ROWS, EZ), F32)
    low, high = lax.fori_loop(0, 16, pack, (zero, zero), unroll=4)
    edge_z[0] = low
    edge_z[1] = high


def entropy_step(held, ent, prim):
    def node(n, carry):
        rho, mx, my, mz, energy = [held[k, n] for k in range(5)]
        inv_rho = 1.0 / rho
        pressure = 0.4 * (energy - 0.5 * (mx * mx + my * my + mz * mz) * inv_rho)
        inv_p = 1.0 / pressure
        ent[n, 0] = mx * inv_p
        ent[n, 1] = my * inv_p
        ent[n, 2] = mz * inv_p
        ent[n, 3] = -rho * inv_p
        prim[n, 0] = mx * inv_rho
        prim[n, 1] = my * inv_rho
        prim[n, 2] = mz * inv_rho
        prim[n, 3] = pressure * inv_rho
        return carry

    lax.fori_loop(0, 64, node, 0, unroll=4)


def fill_edges(edges, near_x):
    edges[:, :, 0:EY, :] = near_x[1]
    edges[:, :, ROWS - EY : ROWS, :] = near_x[0]


def flux_step(ent, prim, near_x, near_z, flux, edges):
    fill_edges(edges, near_x)

    def lines(i, carry):
        low, high = carry
        for comp in range(4):
            for a, value in enumerate(x_line(ent, i, comp, edges)):
                flux[16 * a + i, comp] = value
            for b, value in enumerate(y_line(ent, i, comp)[1]):
                flux[16 * (i // 4) + 4 * b + i % 4, 4 + comp] = value
            outs = z_line(ent, i, comp, low[:, comp : comp + 1], high[:, comp : comp + 1])
            for c, value in enumerate(outs):
                flux[4 * i + c, 8 + comp] = value
        return pltpu.roll(low, EZ - 4, 1), pltpu.roll(high, EZ - 4, 1)

    lax.fori_loop(0, 16, lines, (near_z[1], near_z[0]))

    def node(n, carry):
        vel = [prim[n, k] for k in range(3)]
        temp = prim[n, 3]
        slope4 = [flux[n, 4 * d + 3] for d in range(3)]
        strain = [
            [temp * (flux[n, 4 * d + i] + vel[i] * slope4[d]) for i in range(3)]
            for d in range(3)
        ]
        bulk = (2.0 / 3.0 * VISCOSITY) * (strain[0][0] + strain[1][1] + strain[2][2])
        heat = FOURIER_LAW_ON * temp * temp
        tau = {}
        for d in range(3):
            for i in range(d, 3):
                entry = VISCOSITY * (strain[d][i] + strain[i][d])
                if i == d:
                    entry = entry - bulk
                tau[d, i] = tau[i, d] = entry
        for d in range(3):
            for i in range(3):
                flux[n, 4 * d + i] = tau[i, d]
            flux[n, 4 * d + 3] = (
                vel[0] * tau[0, d] + vel[1] * tau[1, d] + vel[2] * tau[2, d] + heat * slope4[d]
            )
        return carry

    lax.fori_loop(0, 64, node, 0, unroll=2)


def rate_step(flux, near_x, near_z, shear, edges, held):
    fill_edges(edges, near_x)

    def lines_x(i, carry):
        for comp in range(4):
            for a, value in enumerate(x_line(flux, i, comp, edges)):
                held[16 * a + i, comp] = value
        return carry

    lax.fori_loop(0, 16, lines_x, 0, unroll=2)
    row = tile_iota(0)

    def lines_y(i, carry):
        for comp in range(4):
            values, outs = y_line(flux, i, 4 + comp)
            if comp in (0, 2):
                wall = jnp.zeros((ROWS, EZ), F32)
                for ex in range(EX):
                    here = shear[comp // 2, pl.ds(EX * i + ex, 1), :]
                    wall = jnp.where(row == EY * ex, 6.0 * (values[0] - here), wall)
                outs[0] = outs[0] + wall
            for b, value in enumerate(outs):
                held[16 * (i // 4) + 4 * b + i % 4, comp] += value
        return carry

    lax.fori_loop(0, 16, lines_y, 0, unroll=2)

    def lines_z(i, carry):
        low, high = carry
        for comp in range(4):
            outs = z_line(flux, i, 8 + comp, low[:, comp : comp + 1], high[:, comp : comp + 1])
            for c, value in enumerate(outs):
                held[4 * i + c, comp] += value
        return pltpu.roll(low, EZ - 4, 1), pltpu.roll(high, EZ - 4, 1)

    lax.fori_loop(0, 16, lines_z, (near_z[1], near_z[0]), unroll=2)


def two_parts(value):
    high = value.astype(BF16)
    return high, (value - high.astype(F32)).astype(BF16)


def hot(rows, index):
    ids = lax.broadcasted_iota(jnp.int32, (rows, index.shape[1]), 0)
    return jnp.where(ids == index, 1.0, 0.0).astype(BF16)


def lanes(ref, first, count):
    return jnp.concatenate([ref[pl.ds(first + j, 1), :] for j in range(count)], axis=1)


def lagrange_rows(coordinate):
    points = gauss_points()
    rows_out = []
    for i in range(4):
        product = None
        scale = 1.0
        for j in range(4):
            if j != i:
                factor = coordinate - float(points[j])
                product = factor if product is None else product * factor
                scale = scale / (points[i] - points[j])
        rows_out.append(product * float(scale))
    return rows_out


def slot_numbers(dest, wall_count, capacity):
    rows = dest.shape[0]
    masks = [jnp.where(dest == w, 1.0, 0.0) for w in range(wall_count)]
    stacked = jnp.concatenate([mask.astype(BF16) for mask in masks], axis=0)
    from_lane = lax.broadcasted_iota(jnp.int32, (LANES, 2 * LANES), 0)
    to_lane = lax.broadcasted_iota(jnp.int32, (LANES, 2 * LANES), 1)
    upper = jnp.where(from_lane < to_lane, 1.0, 0.0).astype(BF16)
    counts = jnp.dot(stacked, upper, preferred_element_type=F32)
    from_row = lax.broadcasted_iota(jnp.int32, (rows, rows), 1)
    to_row = lax.broadcasted_iota(jnp.int32, (rows, rows), 0)
    below = jnp.where(from_row < to_row, 1.0, 0.0).astype(BF16)
    rank = jnp.zeros(dest.shape, F32)
    for w in range(wall_count):
        part = counts[w * rows : (w + 1) * rows]
        earlier = jnp.dot(below, part[:, LANES:].astype(BF16), preferred_element_type=F32)
        rank = rank + masks[w] * (part[:, :LANES] + earlier)
    return dest * capacity + rank.astype(jnp.int32)


def wall_model(mass_per_volume, mom_x, mom_z, height, factor):
    vel_x = mom_x / mass_per_volume
    vel_z = mom_z / mass_per_volume
    slip_speed = jnp.maximum(jnp.sqrt(vel_x * vel_x + vel_z * vel_z), 0.5)
    reynolds = height * slip_speed * mass_per_volume / VISCOSITY
    log_term = jnp.log(factor * reynolds)
    ratio = jnp.ones_like(mass_per_volume)
    for sweep_index in range(NEWTON):
        residue = ratio - (log_term - jnp.log(ratio)) / KARMAN
        newton_slope = 1.0 + 1.0 / (KARMAN * ratio)
        ratio = ratio - RELAXATION * residue / newton_slope
    friction = slip_speed / ratio
    stress_scale = mass_per_volume * friction * friction / slip_speed
    return (stress_scale * vel_x, stress_scale * vel_z)


def split_columns(columns, parts):
    for k in range(3):
        high, low = two_parts(columns[k])
        parts[64 * k : 64 * k + 64] = high
        parts[192 + 64 * k : 256 + 64 * k] = low


def probe_step(begin, end, elem, coord, table, slots, parts, probe):
    elems = parts.shape[1]
    grid_rows = table.shape[0] // 2
    group = WIDTH // LANES

    def probe_block(t, carry):
        first = group * t
        element = lanes(elem, first, group)
        slot = lanes(slots, first, group)
        coords = coord[:, pl.ds(pl.multiple_of(t * WIDTH, WIDTH), WIDTH)]
        coords = (2.0 * coords.astype(F32) + 1.0) / RES - 1.0
        inner = hot(LANES, element % LANES)
        pieces = []
        for g in range(elems // LANES):
            pick = jnp.where(element // LANES == g, 1.0, 0.0).astype(BF16)
            pieces.append(inner * pick)
        element_hot = jnp.concatenate(pieces, axis=0)
        picked = jnp.dot(parts[...], element_hot, preferred_element_type=F32)
        picked = picked[:192] + picked[192:]
        basis = lagrange_rows(coords)
        along_z = jnp.concatenate([basis[c][2:3] for c in range(4)], axis=0)
        plane = jnp.concatenate([basis[b][1:2] * along_z for b in range(4)], axis=0)
        outs = []
        for k in range(3):
            mixed = basis[0][0:1] * picked[64 * k : 64 * k + 16]
            for a in range(1, 4):
                mixed = mixed + basis[a][0:1] * picked[64 * k + 16 * a : 64 * k + 16 * a + 16]
            outs.append(jnp.sum(mixed * plane, axis=0, keepdims=True))
        layer = (element // EZ % EY).astype(F32)
        outs.append(2.0 * layer + 1.0 + coords[1:2])
        found = jnp.dot(table, hot(LANES, slot % LANES), preferred_element_type=F32)
        found = found[:grid_rows] + found[grid_rows:]
        ids = lax.broadcasted_iota(jnp.int32, (grid_rows, WIDTH), 0)
        outs.append(
            jnp.sum(jnp.where(ids == slot // LANES, found, 0.0), axis=0, keepdims=True)
        )
        for k, value in enumerate(outs):
            for j in range(group):
                probe[k, pl.ds(first + j, 1), :] = value[:, LANES * j : LANES * (j + 1)]
        return carry

    lax.fori_loop(begin, end, probe_block, 0)


def scatter_step(slots, shear, total, outgoing):
    grid_rows = total.shape[0] // 4
    group = WIDTH // LANES
    total[...] = jnp.zeros_like(total)

    def scatter_block(t, carry):
        first = group * t
        slot = lanes(slots, first, group)
        owner = hot(grid_rows, slot // LANES)
        left = []
        for s in range(2):
            for part in two_parts(lanes(shear.at[s], first, group)):
                left.append(owner * part)
        total[...] += lax.dot_general(
            jnp.concatenate(left, axis=0),
            hot(LANES, slot % LANES),
            (((1,), (1,)), ((), ())),
            preferred_element_type=F32,
        )
        return carry

    lax.fori_loop(0, slots.shape[0] // group, scatter_block, 0)
    for s in range(2):
        base = 2 * s * grid_rows
        both = total[base : base + grid_rows] + total[base + grid_rows : base + 2 * grid_rows]
        outgoing[s] = both.reshape(outgoing.shape[1:])


def step_kernel(
    wall_count, slab_count, flow, elem, coord, dest, rough, rate, shear_out,
    held, columns, ent, prim, flux, rate_held, edges, edge_x, edge_z, near_x, near_z,
    blocks, arrived, parts, slots, probe, shear, total, outgoing, landed,
    flow_sems, rate_sems, edge_send, edge_recv, rough_send, rough_recv, shear_send, shear_recv,
):
    slab = lax.axis_index("slab")
    wall = lax.axis_index("wall")
    slab_next = lax.rem(slab + 1, slab_count)
    slab_prev = lax.rem(slab + slab_count - 1, slab_count)
    wall_next = lax.rem(wall + 1, wall_count)
    wall_prev = lax.rem(wall + wall_count - 1, wall_count)
    share = rough.shape[0] // wall_count
    padded = blocks.shape[1]
    flow_copies = [
        pltpu.make_async_copy(
            flow.at[:, :, pl.ds(k * EZ, EZ)], held.at[:, :, k, :], flow_sems.at[k]
        )
        for k in range(ROWS)
    ]
    column_copies = [
        pltpu.make_async_copy(flow.at[comp], columns.at[k], flow_sems.at[ROWS + k])
        for k, comp in enumerate((0, 1, 3))
    ]
    for copy in flow_copies + column_copies:
        copy.start()
    barrier = pltpu.get_barrier_semaphore()
    peers = [{"slab": slab_next}, {"slab": slab_prev}]
    peers += [{"wall": lax.rem(wall + d, wall_count)} for d in range(1, wall_count)]
    for peer in peers:
        pl.semaphore_signal(barrier, inc=1, device_id=peer, device_id_type=MESH)
    blocks[...] = jnp.zeros_like(blocks)
    for w in range(wall_count):
        blocks[w, 0:share, :] = rough[w * share : (w + 1) * share, :]
    pl.semaphore_wait(barrier, len(peers))

    def remote(source, target, send, recv, peer):
        return pltpu.make_async_remote_copy(
            src_ref=source, dst_ref=target, send_sem=send, recv_sem=recv,
            device_id=peer, device_id_type=MESH,
        )

    rough_copies = []
    for d in range(1, wall_count):
        peer = lax.rem(wall + d, wall_count)
        rough_copies.append(
            remote(
                blocks.at[peer], arrived.at[wall], rough_send.at[d], rough_recv.at[d],
                {"wall": peer},
            )
        )
    for copy in rough_copies:
        copy.start()
    arrived[wall] = blocks[wall]

    def send_edges(phase):
        copies = []
        for k, (buffer, near, axis, peers_of) in enumerate(
            (
                (edge_x, near_x, "slab", (slab_prev, slab_next)),
                (edge_z, near_z, "wall", (wall_prev, wall_next)),
            )
        ):
            for side in range(2):
                copies.append(
                    remote(
                        buffer.at[phase, side], near.at[phase, side],
                        edge_send.at[phase, 2 * k + side], edge_recv.at[phase, 2 * k + side],
                        {axis: peers_of[side]},
                    )
                )
        for copy in copies:
            copy.start()
        return copies

    for copy in flow_copies:
        copy.wait()
    entropy_step(held, ent, prim)
    write_edges(ent, 0, 0, edge_x.at[0], edge_z.at[0])
    edge_copies = send_edges(0)
    slots[...] = slot_numbers(dest[...], wall_count, padded * LANES)
    for copy in column_copies:
        copy.wait()
    split_columns(columns, parts)
    for copy in rough_copies:
        copy.wait()
    table = jnp.concatenate(two_parts(arrived[...].reshape(wall_count * padded, LANES)), axis=0)
    steps = slots.shape[0] * LANES // WIDTH
    first = steps // 4
    probe_step(0, first, elem, coord, table, slots, parts, probe)
    for copy in edge_copies:
        copy.wait()
    flux_step(ent, prim, near_x.at[0], near_z.at[0], flux, edges)
    write_edges(flux, 0, 8, edge_x.at[1], edge_z.at[1])
    edge_copies = send_edges(1)
    probe_step(first, steps, elem, coord, table, slots, parts, probe)
    stress = wall_model(probe[0], probe[1], probe[2], probe[3], probe[4])
    shear[0] = stress[0]
    shear[1] = stress[1]
    scatter_step(slots, shear, total, outgoing)
    shear_copies = []
    for d in range(1, wall_count):
        peer = lax.rem(wall + d, wall_count)
        shear_copies.append(
            remote(
                outgoing.at[:, peer], landed.at[:, wall], shear_send.at[d], shear_recv.at[d],
                {"wall": peer},
            )
        )
    for copy in shear_copies:
        copy.start()
    for s in range(2):
        landed[s, wall] = outgoing[s, wall]
    for copy in edge_copies:
        copy.wait()
    rate_step(flux, near_x.at[1], near_z.at[1], shear, edges, rate_held)
    rate_copies = [
        pltpu.make_async_copy(
            rate_held.at[:, :, k, :], rate.at[:, :, pl.ds(k * EZ, EZ)], rate_sems.at[k]
        )
        for k in range(ROWS)
    ]
    for copy in rate_copies:
        copy.start()
    for copy in shear_copies:
        copy.wait()
    for s in range(2):
        for w in range(wall_count):
            shear_out[w * share : (w + 1) * share, s, :] = landed[s, w, 0:share, :]
    for copy in rate_copies:
        copy.wait()


def shape(*dims):
    return jax.ShapeDtypeStruct(dims, F32)


def local(flow_state, match_elem, match_coord, match_dest, roughness):
    wall_count = lax.axis_size("wall")
    slab_count = lax.axis_size("slab")
    rows = match_elem.shape[0] // LANES
    grid_rows = roughness.shape[0] // LANES
    padded = -(-(grid_rows // wall_count) // 8) * 8
    elems = flow_state.shape[2]
    tiles = (ROWS, EZ)
    dma = pltpu.SemaphoreType.DMA
    rate, wall_shear = pl.pallas_call(
        lambda *refs: step_kernel(wall_count, slab_count, *refs),
        out_shape=(shape(64, 4, elems), shape(grid_rows, 2, LANES)),
        in_specs=[ANY] + [VMEM] * 4,
        out_specs=(ANY, VMEM),
        scratch_shapes=[
            pltpu.VMEM((5, 64) + tiles, F32),
            pltpu.VMEM((3, 64, elems), F32),
            pltpu.VMEM((64, 4) + tiles, F32),
            pltpu.VMEM((64, 4) + tiles, F32),
            pltpu.VMEM((64, 12) + tiles, F32),
            pltpu.VMEM((64, 4) + tiles, F32),
            pltpu.VMEM((16, 4) + tiles, F32),
            pltpu.VMEM((2, 2, 16, 4, EY, EZ), F32),
            pltpu.VMEM((2, 2) + tiles, F32),
            pltpu.VMEM((2, 2, 16, 4, EY, EZ), F32),
            pltpu.VMEM((2, 2) + tiles, F32),
            pltpu.VMEM((wall_count, padded, LANES), F32),
            pltpu.VMEM((wall_count, padded, LANES), F32),
            pltpu.VMEM((384, elems), BF16),
            pltpu.VMEM((rows, LANES), jnp.int32),
            pltpu.VMEM((5, rows, LANES), F32),
            pltpu.VMEM((2, rows, LANES), F32),
            pltpu.VMEM((4 * wall_count * padded, LANES), F32),
            pltpu.VMEM((2, wall_count, padded, LANES), F32),
            pltpu.VMEM((2, wall_count, padded, LANES), F32),
            dma((ROWS + 3,)),
            dma((ROWS,)),
            dma((2, 4)),
            dma((2, 4)),
            dma((wall_count,)),
            dma((wall_count,)),
            dma((wall_count,)),
            dma((wall_count,)),
        ],
        compiler_params=pltpu.CompilerParams(
            vmem_limit_bytes=48 * 2**20, collective_id=0, has_side_effects=True
        ),
        cost_estimate=pl.CostEstimate(
            flops=2 * 384 * elems * rows * LANES, bytes_accessed=4 * 576 * elems, transcendentals=0
        ),
        name="residual_step",
    )(
        flow_state.transpose(1, 0, 2),
        match_elem.reshape(rows, LANES),
        match_coord,
        match_dest.reshape(rows, LANES),
        roughness.reshape(grid_rows, LANES),
    )
    return (rate, wall_shear.transpose(1, 0, 2).reshape(2, grid_rows * LANES))


def solution(mesh):
    return jax.shard_map(
        local,
        mesh=mesh,
        in_specs=(
            P(None, None, ("slab", "wall")),
            P(("slab", "wall")),
            P(None, ("slab", "wall")),
            P(("slab", "wall"), None),
            P(("slab", "wall")),
        ),
        out_specs=(P(None, None, ("slab", "wall")), P(None, ("slab", "wall"))),
        check_vma=False,
    )
```

```python
import jax
import jax.numpy as jnp
import numpy as np
from jax import lax
from jax.experimental import pallas as pl
from jax.experimental.pallas import tpu as pltpu
from jax.sharding import PartitionSpec as P

EX = 4
EY = 2
EZ = 128
ROWS = EX * EY
RES = 16
NEWTON = 8
LANES = 128
WIDTH = 2048
VISCOSITY = 0.05
FOURIER_LAW_ON = 0.07 / 0.288
KARMAN = 0.41
RELAXATION = 0.35
F32 = jnp.float32
BF16 = jnp.bfloat16
MESH = pl.DeviceIdType.MESH
VMEM = pl.BlockSpec(memory_space=pltpu.VMEM)
ANY = pl.BlockSpec(memory_space=pl.ANY)
HBM = pl.BlockSpec(memory_space=pltpu.HBM)


def gauss_points():
    return np.array([-1.0, -1.0 / np.sqrt(5.0), 1.0 / np.sqrt(5.0), 1.0])


def derivative_matrix():
    points = gauss_points()
    weights = [
        1.0 / np.prod([points[i] - points[j] for j in range(4) if j != i]) for i in range(4)
    ]
    matrix = np.zeros((4, 4))
    for i in range(4):
        for j in range(4):
            if j != i:
                matrix[i, j] = weights[j] / weights[i] / (points[i] - points[j])
        matrix[i, i] = -np.sum(matrix[i])
    return matrix


TABLE = derivative_matrix() + np.diag([3.0, 0.0, 0.0, -3.0])


def line_slopes(values, prev_upper, next_lower):
    outs = []
    for i in range(4):
        total = None
        for j in range(4):
            coef = float(TABLE[i, j])
            if abs(coef) > 1e-12:
                term = coef * values[j]
                total = term if total is None else total + term
        if i == 0:
            total = total - 3.0 * prev_upper
        if i == 3:
            total = total + 3.0 * next_lower
        outs.append(total)
    return outs


def tile_iota(axis):
    return lax.broadcasted_iota(jnp.int32, (ROWS, EZ), axis)


def x_line(source, i, comp, edges):
    row = tile_iota(0)
    values = [source[16 * a + i, comp] for a in range(4)]
    edge = edges[i, comp % 4]
    prev_upper = jnp.where(row < EY, edge, pltpu.roll(values[3], EY, 0))
    next_lower = jnp.where(row >= ROWS - EY, edge, pltpu.roll(values[0], ROWS - EY, 0))
    return line_slopes(values, prev_upper, next_lower)


def y_line(source, i, comp):
    layer = tile_iota(0) % EY
    base = 16 * (i // 4) + i % 4
    values = [source[base + 4 * b, comp] for b in range(4)]
    prev_upper = jnp.where(layer > 0, pltpu.roll(values[3], 1, 0), values[0])
    next_lower = jnp.where(layer < EY - 1, pltpu.roll(values[0], ROWS - 1, 0), values[3])
    return values, line_slopes(values, prev_upper, next_lower)


def z_line(source, i, comp, low, high):
    lane = tile_iota(1)
    values = [source[4 * i + c, comp] for c in range(4)]
    prev_upper = jnp.where(lane == 0, low, pltpu.roll(values[3], 1, 1))
    next_lower = jnp.where(lane == EZ - 1, high, pltpu.roll(values[0], EZ - 1, 1))
    return line_slopes(values, prev_upper, next_lower)


def write_edges(source, comp_x, comp_z, edge_x, edge_z):
    edge_x[0] = source[0:16, comp_x : comp_x + 4, 0:EY, :]
    edge_x[1] = source[48:64, comp_x : comp_x + 4, ROWS - EY : ROWS, :]
    lane = tile_iota(1)

    def pack(i, carry):
        low, high = carry
        for comp in range(4):
            here = lane == 4 * i + comp
            low = jnp.where(here, source[4 * i, comp_z + comp][:, 0:1], low)
            high = jnp.where(here, source[4 * i + 3, comp_z + comp][:, EZ - 1 : EZ], high)
        return low, high

    zero = jnp.zeros((ROWS, EZ), F32)
    low, high = lax.fori_loop(0, 16, pack, (zero, zero), unroll=4)
    edge_z[0] = low
    edge_z[1] = high


def entropy_step(held, ent, prim):
    def node(n, carry):
        rho, mx, my, mz, energy = [held[k, n] for k in range(5)]
        inv_rho = 1.0 / rho
        pressure = 0.4 * (energy - 0.5 * (mx * mx + my * my + mz * mz) * inv_rho)
        inv_p = 1.0 / pressure
        ent[n, 0] = mx * inv_p
        ent[n, 1] = my * inv_p
        ent[n, 2] = mz * inv_p
        ent[n, 3] = -rho * inv_p
        prim[n, 0] = mx * inv_rho
        prim[n, 1] = my * inv_rho
        prim[n, 2] = mz * inv_rho
        prim[n, 3] = pressure * inv_rho
        return carry

    lax.fori_loop(0, 64, node, 0, unroll=4)


def fill_edges(edges, near_x):
    edges[:, :, 0:EY, :] = near_x[1]
    edges[:, :, ROWS - EY : ROWS, :] = near_x[0]


def flux_step(ent, prim, near_x, near_z, flux, edges):
    fill_edges(edges, near_x)

    def lines(i, carry):
        low, high = carry
        for comp in range(4):
            for a, value in enumerate(x_line(ent, i, comp, edges)):
                flux[16 * a + i, comp] = value
            for b, value in enumerate(y_line(ent, i, comp)[1]):
                flux[16 * (i // 4) + 4 * b + i % 4, 4 + comp] = value
            outs = z_line(ent, i, comp, low[:, comp : comp + 1], high[:, comp : comp + 1])
            for c, value in enumerate(outs):
                flux[4 * i + c, 8 + comp] = value
        return pltpu.roll(low, EZ - 4, 1), pltpu.roll(high, EZ - 4, 1)

    lax.fori_loop(0, 16, lines, (near_z[1], near_z[0]))

    def node(n, carry):
        vel = [prim[n, k] for k in range(3)]
        temp = prim[n, 3]
        slope4 = [flux[n, 4 * d + 3] for d in range(3)]
        strain = [
            [temp * (flux[n, 4 * d + i] + vel[i] * slope4[d]) for i in range(3)]
            for d in range(3)
        ]
        bulk = (2.0 / 3.0 * VISCOSITY) * (strain[0][0] + strain[1][1] + strain[2][2])
        heat = FOURIER_LAW_ON * temp * temp
        tau = {}
        for d in range(3):
            for i in range(d, 3):
                entry = VISCOSITY * (strain[d][i] + strain[i][d])
                if i == d:
                    entry = entry - bulk
                tau[d, i] = tau[i, d] = entry
        for d in range(3):
            for i in range(3):
                flux[n, 4 * d + i] = tau[i, d]
            flux[n, 4 * d + 3] = (
                vel[0] * tau[0, d] + vel[1] * tau[1, d] + vel[2] * tau[2, d] + heat * slope4[d]
            )
        return carry

    lax.fori_loop(0, 64, node, 0, unroll=2)


def rate_step(flux, near_x, near_z, shear, edges, held):
    fill_edges(edges, near_x)

    def lines_x(i, carry):
        for comp in range(4):
            for a, value in enumerate(x_line(flux, i, comp, edges)):
                held[16 * a + i, comp] = value
        return carry

    lax.fori_loop(0, 16, lines_x, 0, unroll=2)
    row = tile_iota(0)

    def lines_y(i, carry):
        for comp in range(4):
            values, outs = y_line(flux, i, 4 + comp)
            if comp in (0, 2):
                wall = jnp.zeros((ROWS, EZ), F32)
                for ex in range(EX):
                    here = shear[comp // 2, pl.ds(EX * i + ex, 1), :]
                    wall = jnp.where(row == EY * ex, 6.0 * (values[0] - here), wall)
                outs[0] = outs[0] + wall
            for b, value in enumerate(outs):
                held[16 * (i // 4) + 4 * b + i % 4, comp] += value
        return carry

    lax.fori_loop(0, 16, lines_y, 0, unroll=2)

    def lines_z(i, carry):
        low, high = carry
        for comp in range(4):
            outs = z_line(flux, i, 8 + comp, low[:, comp : comp + 1], high[:, comp : comp + 1])
            for c, value in enumerate(outs):
                held[4 * i + c, comp] += value
        return pltpu.roll(low, EZ - 4, 1), pltpu.roll(high, EZ - 4, 1)

    lax.fori_loop(0, 16, lines_z, (near_z[1], near_z[0]), unroll=2)


def two_parts(value):
    high = value.astype(BF16)
    return high, (value - high.astype(F32)).astype(BF16)


def hot(rows, index):
    ids = lax.broadcasted_iota(jnp.int32, (rows, index.shape[1]), 0)
    return jnp.where(ids == index, 1.0, 0.0).astype(BF16)


def lanes(ref, first, count):
    return jnp.concatenate([ref[pl.ds(first + j, 1), :] for j in range(count)], axis=1)


def lagrange_rows(coordinate):
    points = gauss_points()
    rows_out = []
    for i in range(4):
        product = None
        scale = 1.0
        for j in range(4):
            if j != i:
                factor = coordinate - float(points[j])
                product = factor if product is None else product * factor
                scale = scale / (points[i] - points[j])
        rows_out.append(product * float(scale))
    return rows_out


def slot_numbers(dest, wall_count, capacity):
    rows = dest.shape[0]
    masks = [jnp.where(dest == w, 1.0, 0.0) for w in range(wall_count)]
    stacked = jnp.concatenate([mask.astype(BF16) for mask in masks], axis=0)
    from_lane = lax.broadcasted_iota(jnp.int32, (LANES, 2 * LANES), 0)
    to_lane = lax.broadcasted_iota(jnp.int32, (LANES, 2 * LANES), 1)
    upper = jnp.where(from_lane < to_lane, 1.0, 0.0).astype(BF16)
    counts = jnp.dot(stacked, upper, preferred_element_type=F32)
    from_row = lax.broadcasted_iota(jnp.int32, (rows, rows), 1)
    to_row = lax.broadcasted_iota(jnp.int32, (rows, rows), 0)
    below = jnp.where(from_row < to_row, 1.0, 0.0).astype(BF16)
    rank = jnp.zeros(dest.shape, F32)
    for w in range(wall_count):
        part = counts[w * rows : (w + 1) * rows]
        earlier = jnp.dot(below, part[:, LANES:].astype(BF16), preferred_element_type=F32)
        rank = rank + masks[w] * (part[:, :LANES] + earlier)
    return dest * capacity + rank.astype(jnp.int32)


def wall_model(mass_per_volume, mom_x, mom_z, height, factor):
    vel_x = mom_x / mass_per_volume
    vel_z = mom_z / mass_per_volume
    slip_speed = jnp.maximum(jnp.sqrt(vel_x * vel_x + vel_z * vel_z), 0.5)
    reynolds = height * slip_speed * mass_per_volume / VISCOSITY
    log_term = jnp.log(factor * reynolds)
    ratio = jnp.ones_like(mass_per_volume)
    for sweep_index in range(NEWTON):
        residue = ratio - (log_term - jnp.log(ratio)) / KARMAN
        newton_slope = 1.0 + 1.0 / (KARMAN * ratio)
        ratio = ratio - RELAXATION * residue / newton_slope
    friction = slip_speed / ratio
    stress_scale = mass_per_volume * friction * friction / slip_speed
    return (stress_scale * vel_x, stress_scale * vel_z)


def split_columns(columns, parts):
    for k in range(3):
        high, low = two_parts(columns[k])
        parts[64 * k : 64 * k + 64] = high
        parts[192 + 64 * k : 256 + 64 * k] = low


def probe_step(begin, end, elem, coord, parts, probe):
    elems = parts.shape[1]
    group = WIDTH // LANES

    def probe_block(t, carry):
        first = group * t
        element = lanes(elem, first, group)
        coords = coord[:, pl.ds(pl.multiple_of(t * WIDTH, WIDTH), WIDTH)]
        coords = (2.0 * coords.astype(F32) + 1.0) / RES - 1.0
        inner = hot(LANES, element % LANES)
        pieces = []
        for g in range(elems // LANES):
            pick = jnp.where(element // LANES == g, 1.0, 0.0).astype(BF16)
            pieces.append(inner * pick)
        element_hot = jnp.concatenate(pieces, axis=0)
        picked = jnp.dot(parts[...], element_hot, preferred_element_type=F32)
        picked = picked[:192] + picked[192:]
        basis = lagrange_rows(coords)
        along_z = jnp.concatenate([basis[c][2:3] for c in range(4)], axis=0)
        plane = jnp.concatenate([basis[b][1:2] * along_z for b in range(4)], axis=0)
        outs = []
        for k in range(3):
            mixed = basis[0][0:1] * picked[64 * k : 64 * k + 16]
            for a in range(1, 4):
                mixed = mixed + basis[a][0:1] * picked[64 * k + 16 * a : 64 * k + 16 * a + 16]
            outs.append(jnp.sum(mixed * plane, axis=0, keepdims=True))
        layer = (element // EZ % EY).astype(F32)
        outs.append(2.0 * layer + 1.0 + coords[1:2])
        for k, value in enumerate(outs):
            for j in range(group):
                probe[k, pl.ds(first + j, 1), :] = value[:, LANES * j : LANES * (j + 1)]
        return carry

    lax.fori_loop(begin, end, probe_block, 0)


def gather_step(table, slots, probe):
    grid_rows = table.shape[0] // 2
    group = WIDTH // LANES

    def gather_block(t, carry):
        first = group * t
        slot = lanes(slots, first, group)
        found = jnp.dot(table, hot(LANES, slot % LANES), preferred_element_type=F32)
        found = found[:grid_rows] + found[grid_rows:]
        ids = lax.broadcasted_iota(jnp.int32, (grid_rows, WIDTH), 0)
        value = jnp.sum(jnp.where(ids == slot // LANES, found, 0.0), axis=0, keepdims=True)
        for j in range(group):
            probe[4, pl.ds(first + j, 1), :] = value[:, LANES * j : LANES * (j + 1)]
        return carry

    lax.fori_loop(0, slots.shape[0] // group, gather_block, 0)


def scatter_step(slots, shear, total, outgoing):
    grid_rows = total.shape[0] // 4
    group = WIDTH // LANES
    total[...] = jnp.zeros_like(total)

    def scatter_block(t, carry):
        first = group * t
        slot = lanes(slots, first, group)
        owner = hot(grid_rows, slot // LANES)
        left = []
        for s in range(2):
            for part in two_parts(lanes(shear.at[s], first, group)):
                left.append(owner * part)
        total[...] += lax.dot_general(
            jnp.concatenate(left, axis=0),
            hot(LANES, slot % LANES),
            (((1,), (1,)), ((), ())),
            preferred_element_type=F32,
        )
        return carry

    lax.fori_loop(0, slots.shape[0] // group, scatter_block, 0)
    for s in range(2):
        base = 2 * s * grid_rows
        both = total[base : base + grid_rows] + total[base + grid_rows : base + 2 * grid_rows]
        outgoing[s] = both.reshape(outgoing.shape[1:])


def step_kernel(
    wall_count, slab_count, flow, elem_in, coord_in, dest_in, rough_in, rate, shear_out,
    elem, coord, dest, rough,
    held, columns, ent, prim, flux, rate_held, edges, edge_x, edge_z, near_x, near_z,
    blocks, arrived, parts, slots, probe, shear, total, outgoing, landed,
    flow_sems, rate_sems, edge_send, edge_recv, rough_send, rough_recv, shear_send, shear_recv,
):
    slab = lax.axis_index("slab")
    wall = lax.axis_index("wall")
    slab_next = lax.rem(slab + 1, slab_count)
    slab_prev = lax.rem(slab + slab_count - 1, slab_count)
    wall_next = lax.rem(wall + 1, wall_count)
    wall_prev = lax.rem(wall + wall_count - 1, wall_count)
    share = rough.shape[0] // wall_count
    padded = blocks.shape[1]
    flow_copies = [
        pltpu.make_async_copy(
            flow.at[:, :, pl.ds(k * EZ, EZ)], held.at[:, :, k, :], flow_sems.at[k]
        )
        for k in range(ROWS)
    ]
    column_copies = [
        pltpu.make_async_copy(flow.at[comp], columns.at[k], flow_sems.at[ROWS + k])
        for k, comp in enumerate((0, 1, 3))
    ]
    small_copies = [
        pltpu.make_async_copy(source, target, flow_sems.at[ROWS + 3 + k])
        for k, (source, target) in enumerate(
            ((rough_in, rough), (dest_in, dest), (elem_in, elem), (coord_in, coord))
        )
    ]
    for copy in small_copies[:1] + flow_copies + small_copies[1:] + column_copies:
        copy.start()
    barrier = pltpu.get_barrier_semaphore()
    peers = [{"slab": slab_next}, {"slab": slab_prev}]
    peers += [{"wall": lax.rem(wall + d, wall_count)} for d in range(1, wall_count)]
    for peer in peers:
        pl.semaphore_signal(barrier, inc=1, device_id=peer, device_id_type=MESH)
    blocks[...] = jnp.zeros_like(blocks)
    small_copies[0].wait()
    for w in range(wall_count):
        blocks[w, 0:share, :] = rough[w * share : (w + 1) * share, :]
    pl.semaphore_wait(barrier, len(peers))

    def remote(source, target, send, recv, peer):
        return pltpu.make_async_remote_copy(
            src_ref=source, dst_ref=target, send_sem=send, recv_sem=recv,
            device_id=peer, device_id_type=MESH,
        )

    rough_copies = []
    for d in range(1, wall_count):
        peer = lax.rem(wall + d, wall_count)
        rough_copies.append(
            remote(
                blocks.at[peer], arrived.at[wall], rough_send.at[d], rough_recv.at[d],
                {"wall": peer},
            )
        )
    for copy in rough_copies:
        copy.start()
    arrived[wall] = blocks[wall]

    def send_edges(phase):
        copies = []
        for k, (buffer, near, axis, peers_of) in enumerate(
            (
                (edge_x, near_x, "slab", (slab_prev, slab_next)),
                (edge_z, near_z, "wall", (wall_prev, wall_next)),
            )
        ):
            for side in range(2):
                copies.append(
                    remote(
                        buffer.at[phase, side], near.at[phase, side],
                        edge_send.at[phase, 2 * k + side], edge_recv.at[phase, 2 * k + side],
                        {axis: peers_of[side]},
                    )
                )
        for copy in copies:
            copy.start()
        return copies

    for copy in flow_copies:
        copy.wait()
    entropy_step(held, ent, prim)
    write_edges(ent, 0, 0, edge_x.at[0], edge_z.at[0])
    edge_copies = send_edges(0)
    for copy in small_copies[1:]:
        copy.wait()
    slots[...] = slot_numbers(dest[...], wall_count, padded * LANES)
    for copy in column_copies:
        copy.wait()
    split_columns(columns, parts)
    steps = slots.shape[0] * LANES // WIDTH
    first = steps // 4
    probe_step(0, first, elem, coord, parts, probe)
    for copy in edge_copies:
        copy.wait()
    flux_step(ent, prim, near_x.at[0], near_z.at[0], flux, edges)
    write_edges(flux, 0, 8, edge_x.at[1], edge_z.at[1])
    edge_copies = send_edges(1)
    probe_step(first, steps, elem, coord, parts, probe)
    for copy in rough_copies:
        copy.wait()
    table = jnp.concatenate(two_parts(arrived[...].reshape(wall_count * padded, LANES)), axis=0)
    gather_step(table, slots, probe)
    stress = wall_model(probe[0], probe[1], probe[2], probe[3], probe[4])
    shear[0] = stress[0]
    shear[1] = stress[1]
    scatter_step(slots, shear, total, outgoing)
    shear_copies = []
    for d in range(1, wall_count):
        peer = lax.rem(wall + d, wall_count)
        shear_copies.append(
            remote(
                outgoing.at[:, peer], landed.at[:, wall], shear_send.at[d], shear_recv.at[d],
                {"wall": peer},
            )
        )
    for copy in shear_copies:
        copy.start()
    for s in range(2):
        landed[s, wall] = outgoing[s, wall]
    for copy in edge_copies:
        copy.wait()
    rate_step(flux, near_x.at[1], near_z.at[1], shear, edges, rate_held)
    rate_copies = [
        pltpu.make_async_copy(
            rate_held.at[:, :, k, :], rate.at[:, :, pl.ds(k * EZ, EZ)], rate_sems.at[k]
        )
        for k in range(ROWS)
    ]
    for copy in rate_copies:
        copy.start()
    for copy in shear_copies:
        copy.wait()
    for s in range(2):
        for w in range(wall_count):
            shear_out[w * share : (w + 1) * share, s, :] = landed[s, w, 0:share, :]
    for copy in rate_copies:
        copy.wait()


def shape(*dims):
    return jax.ShapeDtypeStruct(dims, F32)


def local(flow_state, match_elem, match_coord, match_dest, roughness):
    wall_count = lax.axis_size("wall")
    slab_count = lax.axis_size("slab")
    rows = match_elem.shape[0] // LANES
    grid_rows = roughness.shape[0] // LANES
    padded = -(-(grid_rows // wall_count) // 8) * 8
    elems = flow_state.shape[2]
    tiles = (ROWS, EZ)
    dma = pltpu.SemaphoreType.DMA
    rate, wall_shear = pl.pallas_call(
        lambda *refs: step_kernel(wall_count, slab_count, *refs),
        out_shape=(shape(64, 4, elems), shape(grid_rows, 2, LANES)),
        in_specs=[ANY] + [HBM] * 4,
        out_specs=(ANY, VMEM),
        scratch_shapes=[
            pltpu.VMEM((rows, LANES), jnp.int32),
            pltpu.VMEM(match_coord.shape, jnp.int32),
            pltpu.VMEM((rows, LANES), jnp.int32),
            pltpu.VMEM((grid_rows, LANES), F32),
            pltpu.VMEM((5, 64) + tiles, F32),
            pltpu.VMEM((3, 64, elems), F32),
            pltpu.VMEM((64, 4) + tiles, F32),
            pltpu.VMEM((64, 4) + tiles, F32),
            pltpu.VMEM((64, 12) + tiles, F32),
            pltpu.VMEM((64, 4) + tiles, F32),
            pltpu.VMEM((16, 4) + tiles, F32),
            pltpu.VMEM((2, 2, 16, 4, EY, EZ), F32),
            pltpu.VMEM((2, 2) + tiles, F32),
            pltpu.VMEM((2, 2, 16, 4, EY, EZ), F32),
            pltpu.VMEM((2, 2) + tiles, F32),
            pltpu.VMEM((wall_count, padded, LANES), F32),
            pltpu.VMEM((wall_count, padded, LANES), F32),
            pltpu.VMEM((384, elems), BF16),
            pltpu.VMEM((rows, LANES), jnp.int32),
            pltpu.VMEM((5, rows, LANES), F32),
            pltpu.VMEM((2, rows, LANES), F32),
            pltpu.VMEM((4 * wall_count * padded, LANES), F32),
            pltpu.VMEM((2, wall_count, padded, LANES), F32),
            pltpu.VMEM((2, wall_count, padded, LANES), F32),
            dma((ROWS + 7,)),
            dma((ROWS,)),
            dma((2, 4)),
            dma((2, 4)),
            dma((wall_count,)),
            dma((wall_count,)),
            dma((wall_count,)),
            dma((wall_count,)),
        ],
        compiler_params=pltpu.CompilerParams(
            vmem_limit_bytes=48 * 2**20, collective_id=0, has_side_effects=True
        ),
        cost_estimate=pl.CostEstimate(
            flops=2 * 384 * elems * rows * LANES, bytes_accessed=4 * 576 * elems, transcendentals=0
        ),
        name="residual_step",
    )(
        flow_state.transpose(1, 0, 2),
        match_elem.reshape(rows, LANES),
        match_coord,
        match_dest.reshape(rows, LANES),
        roughness.reshape(grid_rows, LANES),
    )
    return (rate, wall_shear.transpose(1, 0, 2).reshape(2, grid_rows * LANES))


def solution(mesh):
    return jax.shard_map(
        local,
        mesh=mesh,
        in_specs=(
            P(None, None, ("slab", "wall")),
            P(("slab", "wall")),
            P(None, ("slab", "wall")),
            P(("slab", "wall"), None),
            P(("slab", "wall")),
        ),
        out_specs=(P(None, None, ("slab", "wall")), P(None, ("slab", "wall"))),
        check_vma=False,
    )
```

```python
import jax
import jax.numpy as jnp
import numpy as np
from jax import lax
from jax.experimental import pallas as pl
from jax.experimental.pallas import tpu as pltpu
from jax.sharding import PartitionSpec as P

EX = 4
EY = 2
EZ = 128
ROWS = EX * EY
RES = 16
NEWTON = 8
LANES = 128
WIDTH = 2048
VISCOSITY = 0.05
FOURIER_LAW_ON = 0.07 / 0.288
KARMAN = 0.41
RELAXATION = 0.35
F32 = jnp.float32
BF16 = jnp.bfloat16
MESH = pl.DeviceIdType.MESH
VMEM = pl.BlockSpec(memory_space=pltpu.VMEM)
ANY = pl.BlockSpec(memory_space=pl.ANY)
HBM = pl.BlockSpec(memory_space=pltpu.HBM)


def gauss_points():
    return np.array([-1.0, -1.0 / np.sqrt(5.0), 1.0 / np.sqrt(5.0), 1.0])


def derivative_matrix():
    points = gauss_points()
    weights = [
        1.0 / np.prod([points[i] - points[j] for j in range(4) if j != i]) for i in range(4)
    ]
    matrix = np.zeros((4, 4))
    for i in range(4):
        for j in range(4):
            if j != i:
                matrix[i, j] = weights[j] / weights[i] / (points[i] - points[j])
        matrix[i, i] = -np.sum(matrix[i])
    return matrix


TABLE = derivative_matrix() + np.diag([3.0, 0.0, 0.0, -3.0])


def line_slopes(values, prev_upper, next_lower):
    outs = []
    for i in range(4):
        total = None
        for j in range(4):
            coef = float(TABLE[i, j])
            if abs(coef) > 1e-12:
                term = coef * values[j]
                total = term if total is None else total + term
        if i == 0:
            total = total - 3.0 * prev_upper
        if i == 3:
            total = total + 3.0 * next_lower
        outs.append(total)
    return outs


def tile_iota(axis):
    return lax.broadcasted_iota(jnp.int32, (ROWS, EZ), axis)


def x_line(source, i, comp, edges):
    row = tile_iota(0)
    values = [source[16 * a + i, comp] for a in range(4)]
    edge = edges[i, comp % 4]
    prev_upper = jnp.where(row < EY, edge, pltpu.roll(values[3], EY, 0))
    next_lower = jnp.where(row >= ROWS - EY, edge, pltpu.roll(values[0], ROWS - EY, 0))
    return line_slopes(values, prev_upper, next_lower)


def y_line(source, i, comp):
    layer = tile_iota(0) % EY
    base = 16 * (i // 4) + i % 4
    values = [source[base + 4 * b, comp] for b in range(4)]
    prev_upper = jnp.where(layer > 0, pltpu.roll(values[3], 1, 0), values[0])
    next_lower = jnp.where(layer < EY - 1, pltpu.roll(values[0], ROWS - 1, 0), values[3])
    return values, line_slopes(values, prev_upper, next_lower)


def z_line(source, i, comp, low, high):
    lane = tile_iota(1)
    values = [source[4 * i + c, comp] for c in range(4)]
    prev_upper = jnp.where(lane == 0, low, pltpu.roll(values[3], 1, 1))
    next_lower = jnp.where(lane == EZ - 1, high, pltpu.roll(values[0], EZ - 1, 1))
    return line_slopes(values, prev_upper, next_lower)


def write_edges(source, comp_x, comp_z, edge_x, edge_z):
    edge_x[0] = source[0:16, comp_x : comp_x + 4, 0:EY, :]
    edge_x[1] = source[48:64, comp_x : comp_x + 4, ROWS - EY : ROWS, :]
    lane = tile_iota(1)

    def pack(i, carry):
        low, high = carry
        for comp in range(4):
            here = lane == 4 * i + comp
            low = jnp.where(here, source[4 * i, comp_z + comp][:, 0:1], low)
            high = jnp.where(here, source[4 * i + 3, comp_z + comp][:, EZ - 1 : EZ], high)
        return low, high

    zero = jnp.zeros((ROWS, EZ), F32)
    low, high = lax.fori_loop(0, 16, pack, (zero, zero), unroll=4)
    edge_z[0] = low
    edge_z[1] = high


def entropy_step(held, ent, prim):
    def node(n, carry):
        rho, mx, my, mz, energy = [held[k, n] for k in range(5)]
        inv_rho = 1.0 / rho
        pressure = 0.4 * (energy - 0.5 * (mx * mx + my * my + mz * mz) * inv_rho)
        inv_p = 1.0 / pressure
        ent[n, 0] = mx * inv_p
        ent[n, 1] = my * inv_p
        ent[n, 2] = mz * inv_p
        ent[n, 3] = -rho * inv_p
        prim[n, 0] = mx * inv_rho
        prim[n, 1] = my * inv_rho
        prim[n, 2] = mz * inv_rho
        prim[n, 3] = pressure * inv_rho
        return carry

    lax.fori_loop(0, 64, node, 0, unroll=4)


def fill_edges(edges, near_x):
    edges[:, :, 0:EY, :] = near_x[1]
    edges[:, :, ROWS - EY : ROWS, :] = near_x[0]


def flux_step(ent, prim, near_x, near_z, flux, edges):
    fill_edges(edges, near_x)

    def lines(i, carry):
        low, high = carry
        for comp in range(4):
            for a, value in enumerate(x_line(ent, i, comp, edges)):
                flux[16 * a + i, comp] = value
            for b, value in enumerate(y_line(ent, i, comp)[1]):
                flux[16 * (i // 4) + 4 * b + i % 4, 4 + comp] = value
            outs = z_line(ent, i, comp, low[:, comp : comp + 1], high[:, comp : comp + 1])
            for c, value in enumerate(outs):
                flux[4 * i + c, 8 + comp] = value
        return pltpu.roll(low, EZ - 4, 1), pltpu.roll(high, EZ - 4, 1)

    lax.fori_loop(0, 16, lines, (near_z[1], near_z[0]))

    def node(n, carry):
        vel = [prim[n, k] for k in range(3)]
        temp = prim[n, 3]
        slope4 = [flux[n, 4 * d + 3] for d in range(3)]
        strain = [
            [temp * (flux[n, 4 * d + i] + vel[i] * slope4[d]) for i in range(3)]
            for d in range(3)
        ]
        bulk = (2.0 / 3.0 * VISCOSITY) * (strain[0][0] + strain[1][1] + strain[2][2])
        heat = FOURIER_LAW_ON * temp * temp
        tau = {}
        for d in range(3):
            for i in range(d, 3):
                entry = VISCOSITY * (strain[d][i] + strain[i][d])
                if i == d:
                    entry = entry - bulk
                tau[d, i] = tau[i, d] = entry
        for d in range(3):
            for i in range(3):
                flux[n, 4 * d + i] = tau[i, d]
            flux[n, 4 * d + 3] = (
                vel[0] * tau[0, d] + vel[1] * tau[1, d] + vel[2] * tau[2, d] + heat * slope4[d]
            )
        return carry

    lax.fori_loop(0, 64, node, 0, unroll=2)


def rate_step(flux, near_x, near_z, shear, edges, held):
    fill_edges(edges, near_x)

    def lines_x(i, carry):
        for comp in range(4):
            for a, value in enumerate(x_line(flux, i, comp, edges)):
                held[16 * a + i, comp] = value
        return carry

    lax.fori_loop(0, 16, lines_x, 0, unroll=2)
    row = tile_iota(0)

    def lines_y(i, carry):
        for comp in range(4):
            values, outs = y_line(flux, i, 4 + comp)
            if comp in (0, 2):
                wall = jnp.zeros((ROWS, EZ), F32)
                for ex in range(EX):
                    here = shear[comp // 2, pl.ds(EX * i + ex, 1), :]
                    wall = jnp.where(row == EY * ex, 6.0 * (values[0] - here), wall)
                outs[0] = outs[0] + wall
            for b, value in enumerate(outs):
                held[16 * (i // 4) + 4 * b + i % 4, comp] += value
        return carry

    lax.fori_loop(0, 16, lines_y, 0, unroll=2)

    def lines_z(i, carry):
        low, high = carry
        for comp in range(4):
            outs = z_line(flux, i, 8 + comp, low[:, comp : comp + 1], high[:, comp : comp + 1])
            for c, value in enumerate(outs):
                held[4 * i + c, comp] += value
        return pltpu.roll(low, EZ - 4, 1), pltpu.roll(high, EZ - 4, 1)

    lax.fori_loop(0, 16, lines_z, (near_z[1], near_z[0]), unroll=2)


def two_parts(value):
    high = value.astype(BF16)
    return high, (value - high.astype(F32)).astype(BF16)


def hot(rows, index):
    ids = lax.broadcasted_iota(jnp.int32, (rows, index.shape[1]), 0)
    return jnp.where(ids == index, 1.0, 0.0).astype(BF16)


def lanes(ref, first, count):
    return jnp.concatenate([ref[pl.ds(first + j, 1), :] for j in range(count)], axis=1)


def lagrange_rows(coordinate):
    points = gauss_points()
    rows_out = []
    for i in range(4):
        product = None
        scale = 1.0
        for j in range(4):
            if j != i:
                factor = coordinate - float(points[j])
                product = factor if product is None else product * factor
                scale = scale / (points[i] - points[j])
        rows_out.append(product * float(scale))
    return rows_out


def slot_numbers(dest, wall_count, capacity):
    rows = dest.shape[0]
    masks = [jnp.where(dest == w, 1.0, 0.0) for w in range(wall_count)]
    stacked = jnp.concatenate([mask.astype(BF16) for mask in masks], axis=0)
    from_lane = lax.broadcasted_iota(jnp.int32, (LANES, 2 * LANES), 0)
    to_lane = lax.broadcasted_iota(jnp.int32, (LANES, 2 * LANES), 1)
    upper = jnp.where(from_lane < to_lane, 1.0, 0.0).astype(BF16)
    counts = jnp.dot(stacked, upper, preferred_element_type=F32)
    from_row = lax.broadcasted_iota(jnp.int32, (rows, rows), 1)
    to_row = lax.broadcasted_iota(jnp.int32, (rows, rows), 0)
    below = jnp.where(from_row < to_row, 1.0, 0.0).astype(BF16)
    rank = jnp.zeros(dest.shape, F32)
    for w in range(wall_count):
        part = counts[w * rows : (w + 1) * rows]
        earlier = jnp.dot(below, part[:, LANES:].astype(BF16), preferred_element_type=F32)
        rank = rank + masks[w] * (part[:, :LANES] + earlier)
    return dest * capacity + rank.astype(jnp.int32)


def wall_model(mass_per_volume, mom_x, mom_z, height, factor):
    vel_x = mom_x / mass_per_volume
    vel_z = mom_z / mass_per_volume
    slip_speed = jnp.maximum(jnp.sqrt(vel_x * vel_x + vel_z * vel_z), 0.5)
    reynolds = height * slip_speed * mass_per_volume / VISCOSITY
    log_term = jnp.log(factor * reynolds)
    ratio = jnp.ones_like(mass_per_volume)
    for sweep_index in range(NEWTON):
        residue = ratio - (log_term - jnp.log(ratio)) / KARMAN
        newton_slope = 1.0 + 1.0 / (KARMAN * ratio)
        ratio = ratio - RELAXATION * residue / newton_slope
    friction = slip_speed / ratio
    stress_scale = mass_per_volume * friction * friction / slip_speed
    return (stress_scale * vel_x, stress_scale * vel_z)


def split_columns(columns, parts):
    for k in range(3):
        high, low = two_parts(columns[k])
        parts[64 * k : 64 * k + 64] = high
        parts[192 + 64 * k : 256 + 64 * k] = low


def probe_step(begin, end, elem, coord, parts, probe):
    elems = parts.shape[1]
    group = WIDTH // LANES

    def probe_block(t, carry):
        first = group * t
        element = lanes(elem, first, group)
        coords = coord[:, pl.ds(pl.multiple_of(t * WIDTH, WIDTH), WIDTH)]
        coords = (2.0 * coords.astype(F32) + 1.0) / RES - 1.0
        inner = hot(LANES, element % LANES)
        pieces = []
        for g in range(elems // LANES):
            pick = jnp.where(element // LANES == g, 1.0, 0.0).astype(BF16)
            pieces.append(inner * pick)
        element_hot = jnp.concatenate(pieces, axis=0)
        picked = jnp.dot(parts[...], element_hot, preferred_element_type=F32)
        picked = picked[:192] + picked[192:]
        basis = lagrange_rows(coords)
        along_z = jnp.concatenate([basis[c][2:3] for c in range(4)], axis=0)
        plane = jnp.concatenate([basis[b][1:2] * along_z for b in range(4)], axis=0)
        outs = []
        for k in range(3):
            mixed = basis[0][0:1] * picked[64 * k : 64 * k + 16]
            for a in range(1, 4):
                mixed = mixed + basis[a][0:1] * picked[64 * k + 16 * a : 64 * k + 16 * a + 16]
            outs.append(jnp.sum(mixed * plane, axis=0, keepdims=True))
        layer = (element // EZ % EY).astype(F32)
        outs.append(2.0 * layer + 1.0 + coords[1:2])
        for k, value in enumerate(outs):
            for j in range(group):
                probe[k, pl.ds(first + j, 1), :] = value[:, LANES * j : LANES * (j + 1)]
        return carry

    lax.fori_loop(begin, end, probe_block, 0)


def gather_step(table, slots, probe):
    grid_rows = table.shape[0] // 2
    group = WIDTH // LANES

    def gather_block(t, carry):
        first = group * t
        slot = lanes(slots, first, group)
        found = jnp.dot(table, hot(LANES, slot % LANES), preferred_element_type=F32)
        found = found[:grid_rows] + found[grid_rows:]
        ids = lax.broadcasted_iota(jnp.int32, (grid_rows, WIDTH), 0)
        value = jnp.sum(jnp.where(ids == slot // LANES, found, 0.0), axis=0, keepdims=True)
        for j in range(group):
            probe[4, pl.ds(first + j, 1), :] = value[:, LANES * j : LANES * (j + 1)]
        return carry

    lax.fori_loop(0, slots.shape[0] // group, gather_block, 0)


def scatter_step(slots, shear, total, outgoing):
    grid_rows = total.shape[0] // 4
    group = WIDTH // LANES
    total[...] = jnp.zeros_like(total)

    def scatter_block(t, carry):
        first = group * t
        slot = lanes(slots, first, group)
        owner = hot(grid_rows, slot // LANES)
        left = []
        for s in range(2):
            for part in two_parts(lanes(shear.at[s], first, group)):
                left.append(owner * part)
        total[...] += lax.dot_general(
            jnp.concatenate(left, axis=0),
            hot(LANES, slot % LANES),
            (((1,), (1,)), ((), ())),
            preferred_element_type=F32,
        )
        return carry

    lax.fori_loop(0, slots.shape[0] // group, scatter_block, 0)
    for s in range(2):
        base = 2 * s * grid_rows
        both = total[base : base + grid_rows] + total[base + grid_rows : base + 2 * grid_rows]
        outgoing[s] = both.reshape(outgoing.shape[1:])


def step_kernel(
    wall_count, slab_count, flow, elem_in, coord_in, dest_in, rough_in, rate, shear_out,
    elem, coord, dest, rough,
    held, columns, ent, prim, flux, rate_held, edges, edge_x, edge_z, near_x, near_z,
    blocks, arrived, parts, slots, probe, shear, total, outgoing, landed,
    flow_sems, rate_sems, edge_send, edge_recv, rough_send, rough_recv, shear_send, shear_recv,
):
    slab = lax.axis_index("slab")
    wall = lax.axis_index("wall")
    slab_next = lax.rem(slab + 1, slab_count)
    slab_prev = lax.rem(slab + slab_count - 1, slab_count)
    wall_next = lax.rem(wall + 1, wall_count)
    wall_prev = lax.rem(wall + wall_count - 1, wall_count)
    share = rough.shape[0] // wall_count
    padded = blocks.shape[1]
    flow_copies = [
        pltpu.make_async_copy(
            flow.at[:, :, pl.ds(k * EZ, EZ)], held.at[:, :, k, :], flow_sems.at[k]
        )
        for k in range(ROWS)
    ]
    column_copies = [
        pltpu.make_async_copy(flow.at[comp], columns.at[k], flow_sems.at[ROWS + k])
        for k, comp in enumerate((0, 1, 3))
    ]
    small_copies = [
        pltpu.make_async_copy(source, target, flow_sems.at[ROWS + 3 + k])
        for k, (source, target) in enumerate(
            ((rough_in, rough), (dest_in, dest), (elem_in, elem), (coord_in, coord))
        )
    ]
    for copy in small_copies[:1] + flow_copies + small_copies[1:] + column_copies:
        copy.start()
    barrier = pltpu.get_barrier_semaphore()
    peers = [{"slab": slab_next}, {"slab": slab_prev}]
    peers += [{"wall": lax.rem(wall + d, wall_count)} for d in range(1, wall_count)]
    for peer in peers:
        pl.semaphore_signal(barrier, inc=1, device_id=peer, device_id_type=MESH)
    blocks[...] = jnp.zeros_like(blocks)
    small_copies[0].wait()
    for w in range(wall_count):
        blocks[w, 0:share, :] = rough[w * share : (w + 1) * share, :]
    pl.semaphore_wait(barrier, len(peers))

    def remote(source, target, send, recv, peer):
        return pltpu.make_async_remote_copy(
            src_ref=source, dst_ref=target, send_sem=send, recv_sem=recv,
            device_id=peer, device_id_type=MESH,
        )

    rough_copies = []
    for d in range(1, wall_count):
        peer = lax.rem(wall + d, wall_count)
        rough_copies.append(
            remote(
                blocks.at[peer], arrived.at[wall], rough_send.at[d], rough_recv.at[d],
                {"wall": peer},
            )
        )
    for copy in rough_copies:
        copy.start()
    arrived[wall] = blocks[wall]

    def send_edges(phase):
        copies = []
        for k, (buffer, near, axis, peers_of) in enumerate(
            (
                (edge_x, near_x, "slab", (slab_prev, slab_next)),
                (edge_z, near_z, "wall", (wall_prev, wall_next)),
            )
        ):
            for side in range(2):
                copies.append(
                    remote(
                        buffer.at[phase, side], near.at[phase, side],
                        edge_send.at[phase, 2 * k + side], edge_recv.at[phase, 2 * k + side],
                        {axis: peers_of[side]},
                    )
                )
        for copy in copies:
            copy.start()
        return copies

    for copy in flow_copies:
        copy.wait()
    entropy_step(held, ent, prim)
    write_edges(ent, 0, 0, edge_x.at[0], edge_z.at[0])
    edge_copies = send_edges(0)
    for copy in small_copies[1:]:
        copy.wait()
    slots[...] = slot_numbers(dest[...], wall_count, padded * LANES)
    for copy in column_copies:
        copy.wait()
    split_columns(columns, parts)
    steps = slots.shape[0] * LANES // WIDTH
    first = steps // 4
    probe_step(0, first, elem, coord, parts, probe)
    for copy in edge_copies:
        copy.wait()
    flux_step(ent, prim, near_x.at[0], near_z.at[0], flux, edges)
    write_edges(flux, 0, 8, edge_x.at[1], edge_z.at[1])
    edge_copies = send_edges(1)
    probe_step(first, steps, elem, coord, parts, probe)
    for copy in rough_copies:
        copy.wait()
    table = jnp.concatenate(two_parts(arrived[...].reshape(wall_count * padded, LANES)), axis=0)
    gather_step(table, slots, probe)
    stress = wall_model(probe[0], probe[1], probe[2], probe[3], probe[4])
    shear[0] = stress[0]
    shear[1] = stress[1]
    scatter_step(slots, shear, total, outgoing)
    shear_copies = []
    for d in range(1, wall_count):
        peer = lax.rem(wall + d, wall_count)
        shear_copies.append(
            remote(
                outgoing.at[:, peer], landed.at[:, wall], shear_send.at[d], shear_recv.at[d],
                {"wall": peer},
            )
        )
    for copy in shear_copies:
        copy.start()
    for s in range(2):
        landed[s, wall] = outgoing[s, wall]
    for copy in edge_copies:
        copy.wait()
    rate_step(flux, near_x.at[1], near_z.at[1], shear, edges, rate_held)
    rate_copies = [
        pltpu.make_async_copy(
            rate_held.at[:, :, k, :], rate.at[:, :, pl.ds(k * EZ, EZ)], rate_sems.at[k]
        )
        for k in range(ROWS)
    ]
    for copy in rate_copies:
        copy.start()
    for copy in shear_copies:
        copy.wait()
    for s in range(2):
        for w in range(wall_count):
            shear_out[w * share : (w + 1) * share, s, :] = landed[s, w, 0:share, :]
    for copy in rate_copies:
        copy.wait()


def shape(*dims):
    return jax.ShapeDtypeStruct(dims, F32)


def local(flow_state, match_elem, match_coord, match_dest, roughness):
    wall_count = lax.axis_size("wall")
    slab_count = lax.axis_size("slab")
    rows = match_elem.shape[0] // LANES
    grid_rows = roughness.shape[0] // LANES
    padded = -(-(grid_rows // wall_count) // 8) * 8
    elems = flow_state.shape[2]
    tiles = (ROWS, EZ)
    dma = pltpu.SemaphoreType.DMA
    rate, wall_shear = pl.pallas_call(
        lambda *refs: step_kernel(wall_count, slab_count, *refs),
        out_shape=(shape(64, 4, elems), shape(grid_rows, 2, LANES)),
        in_specs=[ANY] + [HBM] * 4,
        out_specs=(ANY, VMEM),
        scratch_shapes=[
            pltpu.VMEM((rows, LANES), jnp.int32),
            pltpu.VMEM(match_coord.shape, jnp.int32),
            pltpu.VMEM((rows, LANES), jnp.int32),
            pltpu.VMEM((grid_rows, LANES), F32),
            pltpu.VMEM((5, 64) + tiles, F32),
            pltpu.VMEM((3, 64, elems), F32),
            pltpu.VMEM((64, 4) + tiles, F32),
            pltpu.VMEM((64, 4) + tiles, F32),
            pltpu.VMEM((64, 12) + tiles, F32),
            pltpu.VMEM((64, 4) + tiles, F32),
            pltpu.VMEM((16, 4) + tiles, F32),
            pltpu.VMEM((2, 2, 16, 4, EY, EZ), F32),
            pltpu.VMEM((2, 2) + tiles, F32),
            pltpu.VMEM((2, 2, 16, 4, EY, EZ), F32),
            pltpu.VMEM((2, 2) + tiles, F32),
            pltpu.VMEM((wall_count, padded, LANES), F32),
            pltpu.VMEM((wall_count, padded, LANES), F32),
            pltpu.VMEM((384, elems), BF16),
            pltpu.VMEM((rows, LANES), jnp.int32),
            pltpu.VMEM((5, rows, LANES), F32),
            pltpu.VMEM((2, rows, LANES), F32),
            pltpu.VMEM((4 * wall_count * padded, LANES), F32),
            pltpu.VMEM((2, wall_count, padded, LANES), F32),
            pltpu.VMEM((2, wall_count, padded, LANES), F32),
            dma((ROWS + 7,)),
            dma((ROWS,)),
            dma((2, 4)),
            dma((2, 4)),
            dma((wall_count,)),
            dma((wall_count,)),
            dma((wall_count,)),
            dma((wall_count,)),
        ],
        compiler_params=pltpu.CompilerParams(
            vmem_limit_bytes=60 * 2**20, collective_id=0, has_side_effects=True
        ),
        cost_estimate=pl.CostEstimate(
            flops=2 * 384 * elems * rows * LANES, bytes_accessed=4 * 576 * elems, transcendentals=0
        ),
        name="residual_step",
    )(
        flow_state.transpose(1, 0, 2),
        match_elem.reshape(rows, LANES),
        match_coord,
        match_dest.reshape(rows, LANES),
        roughness.reshape(grid_rows, LANES),
    )
    return (rate, wall_shear.transpose(1, 0, 2).reshape(2, grid_rows * LANES))


def solution(mesh):
    return jax.shard_map(
        local,
        mesh=mesh,
        in_specs=(
            P(None, None, ("slab", "wall")),
            P(("slab", "wall")),
            P(None, ("slab", "wall")),
            P(("slab", "wall"), None),
            P(("slab", "wall")),
        ),
        out_specs=(P(None, None, ("slab", "wall")), P(None, ("slab", "wall"))),
        check_vma=False,
    )
```
